32 devices in a mesh: group: 2 (over y), row: 2 (over core), col: 8 (over z, x).
Axes of the slice: x: 2, y: 2, z: 4, core: 2. Of those that a mesh axis runs over, the one named last changes fastest.
Arguments:
- queries: bfloat16 [32, 256, 576], P(('group', 'col')), parts along dimension 0, may hold values from -64 to 64
- prefix_kv: bfloat16 [8192, 576], P(('group', 'row', 'col')), parts along dimension 0, may hold values from -7 to 7
- suffix_kv: bfloat16 [32, 2048, 576], P(('group', 'col'), 'row'), parts along dimension 0, may hold values from -6 to 6
- lengths: int32 [32], P(('group', 'col')), parts along dimension 0, may hold values from 2 to 2048, as said below
Outputs:
- attended: bfloat16 [32, 256, 512], P(('group', 'col')), parts along dimension 0
The draws below stay inside these ranges and needn't reach their ends.
There are 2 independent parts, one for each index of `group`. The reference program is written for one: setup_inputs(seed, part) draws one part's arguments, and reference() takes and returns one part's arrays. A program takes and returns all parts, laid end to end along the dimension named above; each array names one. Nothing has to cross between parts.
Inputs may be any that keep to these rules, and one draw needn't show every extreme that they name: lengths count a request's 2 new tokens, which are its last used slots; some request has exactly 2048.
All inputs are finite; a program needn't handle non-finite values.
Results may differ from the reference program's by a relative error of at most 0.0065.
Values may be sent and summed in bfloat16 or wider, within the bound.
A program may use at most 128 MiB of HBM per device.

```python
import jax
import jax.numpy as jnp
from jax import lax

H = 128
KVR = 512
LAT = 576
POS = 2
QROWS = 256
REQUESTS = 16
PREFIX = 4096
SUF = 2048


def latent_table(key):
    return jnp.clip(jax.random.normal(jax.random.fold_in(key, 11), (PREFIX, LAT), jnp.float32), -6.0, 6.0)


def draw_prefix_kv(key, part):
    table = latent_table(key)
    return table.astype(jnp.bfloat16)


def draw_queries(key, part):
    own_key = jax.random.fold_in(key, 17)
    queries = jnp.clip(jax.random.normal(own_key, (REQUESTS, QROWS, LAT), jnp.float32), -6.0, 6.0) * 1.6
    return queries.astype(jnp.bfloat16)


def draw_lengths(key, part):
    key = jax.random.fold_in(key, 23)
    lengths = jax.random.randint(jax.random.fold_in(key, 1), (REQUESTS,), POS, SUF + 1)
    chosen = jax.random.randint(jax.random.fold_in(key, 2), (), 0, REQUESTS)
    return lengths.at[chosen].set(SUF).astype(jnp.int32)


def level_of(key, dims, pieces, low, high):
    gain, own = 1.0, jax.random.fold_in(key, 6)
    for axis_at, parts in pieces:
        heights = jnp.exp(jax.random.uniform(jax.random.fold_in(own, axis_at), (parts,), jnp.float32, low / len(pieces), high / len(pieces)))
        gain = gain * jnp.repeat(heights, dims[axis_at] // parts).reshape([-1 if axis == axis_at else 1 for axis in range(len(dims))])
    return gain


def gaussian(stream_key, extent, scale, reach, cuts=(), kind=jnp.bfloat16):
    values = scale * jax.random.normal(stream_key, extent, jnp.float32)
    if cuts:
        values = values * level_of(stream_key, extent, cuts, -0.22, 0.18)
    return jnp.clip(values, -reach, reach).astype(kind)


def setup_inputs(seed: int = 0, part: int = 0) -> dict:
    key_of = jax.random.split(jax.random.key(seed), 5)
    part_splits = jax.random.split(jax.random.fold_in(key_of[4], part), 5)
    queries = draw_queries(jax.random.fold_in(jax.random.fold_in(key_of[4], part), 71), part)
    prefix_kv = draw_prefix_kv(jax.random.fold_in(jax.random.fold_in(key_of[4], part), 71), part)
    suffix_kv = gaussian(part_splits[2], (REQUESTS, SUF, LAT), 1.0, 6.0, ((0, 8), (1, 2)))
    lengths = draw_lengths(jax.random.fold_in(jax.random.fold_in(key_of[4], part), 71), part)
    return dict(queries=queries, prefix_kv=prefix_kv, suffix_kv=suffix_kv, lengths=lengths)


softmax_scale = 192.0 ** -0.5
floor_value = -1e30


def reference(queries, prefix_kv, suffix_kv, lengths):
    key_index = jnp.arange(SUF, dtype=jnp.int32)
    position = jnp.arange(QROWS, dtype=jnp.int32) // H

    def attend_one(request_data):
        query_rows, suffix, length = request_data
        all_keys = jnp.concatenate([prefix_kv, suffix], axis=0)
        scores = jnp.dot(query_rows, all_keys.T, preferred_element_type=jnp.float32) * softmax_scale
        key_limit = length - POS + 1 + position
        visible = key_index[None, :] < key_limit[:, None]
        visible = jnp.concatenate([jnp.ones((QROWS, PREFIX), dtype=bool), visible], axis=1)
        scores = jnp.where(visible, scores, floor_value)
        row_max = jnp.max(scores, axis=1, keepdims=True)
        weights = jnp.where(visible, jnp.exp(scores - row_max), 0.0)
        row_sum = jnp.sum(weights, axis=1, keepdims=True)
        blended = jnp.dot(weights.astype(jnp.bfloat16), all_keys[:, :KVR], preferred_element_type=jnp.float32)
        return (blended / row_sum).astype(jnp.bfloat16)

    return lax.map(attend_one, (queries, suffix_kv, lengths))
```

```python
import math

import jax
import jax.numpy as jnp
from jax import lax
from jax.experimental import pallas as pl
from jax.experimental.pallas import tpu as pltpu
from jax.sharding import PartitionSpec as P

H = 128
KVR = 512
POS = 2


softmax_scale = 192.0 ** (-0.5)
floor_value = -1e30


def merged(value, axis, join):
    pieces = jax.tree.map(lambda part: lax.all_gather(part, axis), value)
    head = jax.tree.map(lambda part: part[0], pieces)
    tail = jax.tree.map(lambda part: part[1:], pieces)
    subtotal, _ = lax.scan(lambda subtotal, share: (join(subtotal, share), None), head, tail)
    return subtotal


def absorb(running, query_flat, key_block):
    maximum, weight_sum, blended = running
    scores = (
        jnp.einsum("ml,kl->mk", query_flat, key_block, preferred_element_type=jnp.float32)
        * softmax_scale
    )
    new_max = jnp.maximum(maximum, jnp.max(scores, axis=1))
    weights = jnp.exp(scores - new_max[:, None])
    rescale = jnp.exp(maximum - new_max)
    weight_sum = weight_sum * rescale + jnp.sum(weights, axis=1)
    blended = blended * rescale[:, None] + jnp.dot(
        weights.astype(jnp.bfloat16), key_block[:, :KVR], preferred_element_type=jnp.float32
    )
    return (new_max, weight_sum, blended)


def sweeper(query_flat, running, key_piece):
    key_count = key_piece.shape[0]
    block_size = math.gcd(key_count, 512)
    pieces = key_piece.reshape(key_count // block_size, block_size, key_piece.shape[1])

    def scan_step(carried, key_block):
        return (absorb(carried, query_flat, key_block), None)

    return lax.scan(scan_step, running, pieces)[0]


def suffix_state(queries_own, suffix, lengths, first_key):
    scores = (
        jnp.einsum("rql,rkl->rqk", queries_own, suffix, preferred_element_type=jnp.float32)
        * softmax_scale
    )
    key_index = first_key + jnp.arange(suffix.shape[1], dtype=jnp.int32)
    position = jnp.arange(queries_own.shape[1], dtype=jnp.int32) // H
    key_limit = lengths[:, None] - POS + 1 + position[None, :]
    visible = key_index[None, None, :] < key_limit[:, :, None]
    scores = jnp.where(visible, scores, floor_value)
    maximum = jnp.max(scores, axis=2)
    weights = jnp.where(visible, jnp.exp(scores - maximum[:, :, None]), 0.0)
    weight_sum = jnp.sum(weights, axis=2)
    blended = jnp.einsum(
        "rqk,rkv->rqv",
        weights.astype(jnp.bfloat16),
        suffix[:, :, :KVR],
        preferred_element_type=jnp.float32,
    )
    flat_rows = queries_own.shape[0] * queries_own.shape[1]
    return (
        maximum.reshape(flat_rows),
        weight_sum.reshape(flat_rows),
        blended.reshape(flat_rows, KVR),
    )


def combine(first, second):
    maximum = jnp.maximum(first[0], second[0])
    scale_first = jnp.exp(first[0] - maximum)
    scale_second = jnp.exp(second[0] - maximum)
    weight_sum = first[1] * scale_first + second[1] * scale_second
    blended = first[2] * scale_first[:, None] + second[2] * scale_second[:, None]
    return (maximum, weight_sum, blended)


def per_device(queries, prefix_kv, suffix_kv, lengths):
    request_count, query_rows, latent_width = queries.shape
    first_key = lax.axis_index("row") * suffix_kv.shape[1]
    softmax_state = suffix_state(queries, suffix_kv, lengths, first_key)
    query_flat = queries.reshape(request_count * query_rows, latent_width)
    softmax_state = sweeper(
        query_flat, softmax_state, lax.all_gather(prefix_kv, "col", axis=0, tiled=True)
    )
    maximum, weight_sum, blended = merged(softmax_state, "row", combine)
    return (
        (blended / weight_sum[:, None]).astype(jnp.bfloat16).reshape(request_count, query_rows, KVR)
    )


END_FIRST = [("near", (0, 0, 0)), ("x", (0, 0, 0)), ("near", (0, 0, 1)), ("x", (0, 0, 1))]
END_EVENTS = [
    ((0, 1, 0), ["x"]),
    ((1, 0, 0), []),
    ((0, 1, 1), []),
    ((1, 0, 1), ["near"]),
    ((0, 2, 0), ["x"]),
    ((1, 1, 0), []),
    ((0, 2, 1), ["x"]),
    ((1, 2, 0), []),
    ((0, 3, 0), ["x"]),
    ((1, 2, 1), []),
    ((0, 3, 1), ["x"]),
    ((1, 3, 0), []),
    ((1, 1, 1), []),
    ((1, 3, 1), []),
]
MID_FIRST = [
    ("near", (0, 1, 0)), ("up", (0, 1, 0)), ("x", (0, 1, 1)),
    ("near", (0, 1, 1)), ("up", (0, 1, 1)), ("x", (0, 1, 0)),
]
MID_EVENTS = [
    ((0, 2, 0), ["near", "x"]),
    ((0, 0, 0), ["up", "x"]),
    ((1, 1, 1), []),
    ((0, 2, 1), ["near"]),
    ((0, 0, 1), ["up", ("up", (1, 1, 1))]),
    ((1, 1, 0), []),
    ((0, 3, 0), ["near", "x"]),
    ((1, 0, 1), []),
    ((1, 0, 0), []),
    ((0, 3, 1), ["near", "x", ("near", (1, 1, 1))]),
    ((1, 2, 0), []),
    ((1, 2, 1), []),
    ((1, 3, 0), []),
    ((1, 3, 1), []),
]
CHUNK = 256
LOG2E = 1.4426950408889634


def dot_t(a, b):
    return lax.dot_general(a, b, (((1,), (1,)), ((), ())), preferred_element_type=jnp.float32)


def gather_attend(
    q_hbm, prefix_hbm, suffix_hbm, lengths, out_hbm,
    q, keys, suffix, result, top, total, acc,
    local_sem, x_send, near_send, up_send, sib_send, recv, sib_recv, suf_send, suf_recv, out_send, out_recv,
):
    group, row, col = lax.axis_index("group"), lax.axis_index("row"), lax.axis_index("col")
    z, x = col // 2, col % 2
    flip = z // 2
    place = z + flip * (3 - 2 * z)
    at_end = place == 0
    unit = prefix_hbm.shape[0] // 2
    half_suffix = suffix_hbm.shape[1]
    other = 1 - row

    def line(p):
        return p + flip * (3 - 2 * p)

    def index(name):
        other_x, p, h = name
        return ((x + other_x - 2 * x * other_x) * 4 + line(p)) * 2 + h

    def slot(u, r):
        return keys.at[u, pl.ds(pl.multiple_of(r * unit, unit), unit), :]

    devices = {
        "x": (group, row, z * 2 + 1 - x),
        "end_near": (group, row, line(1) * 2 + x),
        "mid_near": (group, row, line(0) * 2 + x),
        "up": (group, row, line(2) * 2 + x),
    }
    sibling = (group, other, col)

    def remote(src, dst, send_sem, recv_sem, device):
        return pltpu.make_async_remote_copy(
            src_ref=src, dst_ref=dst, send_sem=send_sem, recv_sem=recv_sem,
            device_id=device, device_id_type=pl.DeviceIdType.MESH,
        )

    barrier = pltpu.get_barrier_semaphore()

    def greet(device):
        pl.semaphore_signal(barrier, inc=1, device_id=device, device_id_type=pl.DeviceIdType.MESH)

    greet(sibling)
    greet(devices["x"])

    q_in = pltpu.make_async_copy(q_hbm.at[row], q, local_sem.at[0])
    q_in.start()
    own_in = []
    for h in range(2):
        own_in.append(
            pltpu.make_async_copy(
                prefix_hbm.at[pl.ds(h * unit, unit), :], slot(index_own(col, h, z, x), row), local_sem.at[1 + h]
            )
        )
        own_in[-1].start()
    suffix_in = pltpu.make_async_copy(
        suffix_hbm.at[row],
        suffix.at[pl.ds(pl.multiple_of(row * half_suffix, half_suffix), half_suffix), :],
        local_sem.at[3],
    )
    suffix_in.start()

    @pl.when(at_end)
    def _():
        greet(devices["end_near"])
        pl.semaphore_wait(barrier, 3)

    @pl.when(jnp.logical_not(at_end))
    def _():
        greet(devices["mid_near"])
        greet(devices["up"])
        pl.semaphore_wait(barrier, 4)

    sems = {"x": x_send, "near": near_send, "up": up_send}

    def make_send(kind, counts, link, name, from_hbm):
        at = counts[link]
        counts[link] += 1
        where = (kind + "_near") if link == "near" else link

        def build():
            u = index(name)
            src = prefix_hbm.at[pl.ds(name[2] * unit, unit), :] if from_hbm else slot(u, row)
            return remote(src, slot(u, row), sems[link].at[at], recv.at[u], devices[where])

        return build

    def plan(kind, first, events):
        counts = {"x": 0, "near": 0, "up": 0}
        opening = [make_send(kind, counts, link, name, True) for link, name in first]
        after = []
        for name, links in events:
            sends = []
            for link in links:
                if isinstance(link, tuple):
                    sends.append(make_send(kind, counts, link[0], link[1], False))
                else:
                    sends.append(make_send(kind, counts, link, name, False))
            after.append(sends)
        return opening, after

    end_opening, end_after = plan("end", END_FIRST, END_EVENTS)
    mid_opening, mid_after = plan("mid", MID_FIRST, MID_EVENTS)

    def both(end_list, mid_list, act):
        if end_list:
            @pl.when(at_end)
            def _():
                for build in end_list:
                    act(build())
        if mid_list:
            @pl.when(jnp.logical_not(at_end))
            def _():
                for build in mid_list:
                    act(build())

    both(end_opening, mid_opening, lambda copy: copy.start())

    sib_sends = []
    own_units = [index_own(col, h, z, x) for h in range(2)]
    for h in range(2):
        copy = remote(
            prefix_hbm.at[pl.ds(h * unit, unit), :], slot(own_units[h], row),
            sib_send.at[h], sib_recv.at[own_units[h]], sibling,
        )
        copy.start()
        sib_sends.append(copy)
    suffix_half = suffix.at[pl.ds(pl.multiple_of(row * half_suffix, half_suffix), half_suffix), :]
    suffix_out = remote(suffix_hbm.at[other], suffix_half, suf_send, suf_recv, sibling)
    suffix_out.start()

    scale = softmax_scale * LOG2E
    top[...] = jnp.full(top.shape, floor_value, jnp.float32)
    total[...] = jnp.zeros(total.shape, jnp.float32)
    acc[...] = jnp.zeros(acc.shape, jnp.float32)
    length = lengths[row]

    def attend(block, first_key=None):
        scores = dot_t(q[...], block) * scale
        if first_key is not None:
            shape = scores.shape
            key = first_key + lax.broadcasted_iota(jnp.int32, shape, 1)
            position = lax.broadcasted_iota(jnp.int32, shape, 0) // H
            scores = jnp.where(key < length - POS + 1 + position, scores, floor_value)
        before = top[...]
        now = jnp.maximum(before, jnp.max(scores, axis=1, keepdims=True))
        weights = jnp.exp2(scores - now)
        rescale = jnp.exp2(before - now)
        top[...] = now
        total[...] = total[...] * rescale + jnp.sum(weights, axis=1, keepdims=True)
        acc[...] = acc[...] * rescale + jnp.dot(
            weights.astype(jnp.bfloat16), block[:, :KVR], preferred_element_type=jnp.float32
        )

    def await_sibling(u):
        remote(slot(u, row), slot(u, other), sib_send.at[0], sib_recv.at[u], sibling).wait_recv()

    pieces = half_suffix // CHUNK

    def attend_suffix(i):
        if i == 0:
            suffix_in.wait()
        if i == pieces:
            remote(
                suffix_half,
                suffix.at[pl.ds(pl.multiple_of(other * half_suffix, half_suffix), half_suffix), :],
                suf_send, suf_recv, sibling,
            ).wait_recv()
        part = row if i < pieces else other
        start = pl.multiple_of(part * half_suffix + (i % pieces) * CHUNK, CHUNK)
        attend(suffix[pl.ds(start, CHUNK), :], start)

    q_in.wait()
    for h in range(2):
        own_in[h].wait()
    for u in own_units:
        await_sibling(u)
        attend(keys[u])

    steps = len(END_EVENTS)
    names = []
    for k in range(steps):
        u = jnp.where(at_end, index(END_EVENTS[k][0]), index(MID_EVENTS[k][0]))
        remote(slot(u, row), slot(u, row), sib_send.at[0], recv.at[u], sibling).wait_recv()
        both(end_after[k], mid_after[k], lambda copy: copy.start())
        copy = remote(slot(u, row), slot(u, row), sib_send.at[2 + k], sib_recv.at[u], sibling)
        copy.start()
        sib_sends.append(copy)
        names.append(u)
        if k < 2 * pieces:
            attend_suffix(k)
        if k >= 1:
            await_sibling(names[k - 1])
            attend(keys[names[k - 1]])
    for i in range(steps, 2 * pieces):
        attend_suffix(i)
    await_sibling(names[-1])
    attend(keys[names[-1]])

    result[...] = (acc[...] / total[...]).astype(jnp.bfloat16)
    final = remote(result, out_hbm.at[row], out_send, out_recv, sibling)
    final.start()
    keep = pltpu.make_async_copy(result, out_hbm.at[row], local_sem.at[4])
    keep.start()
    both(
        end_opening + [b for sends in end_after for b in sends],
        mid_opening + [b for sends in mid_after for b in sends],
        lambda copy: copy.wait_send(),
    )
    for copy in sib_sends:
        copy.wait_send()
    suffix_out.wait_send()
    keep.wait()
    final.wait_send()
    remote(result, out_hbm.at[other], out_send, out_recv, sibling).wait_recv()


def index_own(col, h, z, x):
    return (x * 4 + z) * 2 + h


def ring_device(queries, prefix_kv, suffix_kv, lengths):
    requests, query_rows, width = queries.shape
    block = prefix_kv.shape[0]
    half_suffix = suffix_kv.shape[1]
    dma = pltpu.SemaphoreType.DMA
    anywhere = pl.BlockSpec(memory_space=pl.ANY)
    return pl.pallas_call(
        gather_attend,
        out_shape=jax.ShapeDtypeStruct((requests, query_rows, KVR), jnp.bfloat16),
        in_specs=[anywhere, anywhere, anywhere, pl.BlockSpec(memory_space=pltpu.SMEM)],
        out_specs=anywhere,
        scratch_shapes=[
            pltpu.VMEM((query_rows, width), jnp.bfloat16),
            pltpu.VMEM((16, block, width), jnp.bfloat16),
            pltpu.VMEM((2 * half_suffix, width), jnp.bfloat16),
            pltpu.VMEM((query_rows, KVR), jnp.bfloat16),
            pltpu.VMEM((query_rows, 1), jnp.float32),
            pltpu.VMEM((query_rows, 1), jnp.float32),
            pltpu.VMEM((query_rows, KVR), jnp.float32),
            dma((5,)), dma((7,)), dma((7,)), dma((5,)), dma((16,)), dma((16,)), dma((16,)),
            dma, dma, dma, dma,
        ],
        compiler_params=pltpu.CompilerParams(
            collective_id=0, has_side_effects=True, vmem_limit_bytes=48 * 1024 * 1024
        ),
    )(queries, prefix_kv, suffix_kv, lengths)


def solution(mesh):
    small = dict(mesh.shape) == {"group": 2, "row": 2, "col": 8}
    return jax.shard_map(
        ring_device if small else per_device,
        mesh=mesh,
        in_specs=(
            P(("group", "col"), None, None),
            P(("group", "row", "col"), None),
            P(("group", "col"), "row", None),
            P(("group", "col")),
        ),
        out_specs=P(("group", "col"), None, None),
        check_vma=False,
    )
```

```python
import math

import jax
import jax.numpy as jnp
from jax import lax
from jax.experimental import pallas as pl
from jax.experimental.pallas import tpu as pltpu
from jax.sharding import PartitionSpec as P

H = 128
KVR = 512
POS = 2


softmax_scale = 192.0 ** (-0.5)
floor_value = -1e30


def merged(value, axis, join):
    pieces = jax.tree.map(lambda part: lax.all_gather(part, axis), value)
    head = jax.tree.map(lambda part: part[0], pieces)
    tail = jax.tree.map(lambda part: part[1:], pieces)
    subtotal, _ = lax.scan(lambda subtotal, share: (join(subtotal, share), None), head, tail)
    return subtotal


def absorb(running, query_flat, key_block):
    maximum, weight_sum, blended = running
    scores = (
        jnp.einsum("ml,kl->mk", query_flat, key_block, preferred_element_type=jnp.float32)
        * softmax_scale
    )
    new_max = jnp.maximum(maximum, jnp.max(scores, axis=1))
    weights = jnp.exp(scores - new_max[:, None])
    rescale = jnp.exp(maximum - new_max)
    weight_sum = weight_sum * rescale + jnp.sum(weights, axis=1)
    blended = blended * rescale[:, None] + jnp.dot(
        weights.astype(jnp.bfloat16), key_block[:, :KVR], preferred_element_type=jnp.float32
    )
    return (new_max, weight_sum, blended)


def sweeper(query_flat, running, key_piece):
    key_count = key_piece.shape[0]
    block_size = math.gcd(key_count, 512)
    pieces = key_piece.reshape(key_count // block_size, block_size, key_piece.shape[1])

    def scan_step(carried, key_block):
        return (absorb(carried, query_flat, key_block), None)

    return lax.scan(scan_step, running, pieces)[0]


def suffix_state(queries_own, suffix, lengths, first_key):
    scores = (
        jnp.einsum("rql,rkl->rqk", queries_own, suffix, preferred_element_type=jnp.float32)
        * softmax_scale
    )
    key_index = first_key + jnp.arange(suffix.shape[1], dtype=jnp.int32)
    position = jnp.arange(queries_own.shape[1], dtype=jnp.int32) // H
    key_limit = lengths[:, None] - POS + 1 + position[None, :]
    visible = key_index[None, None, :] < key_limit[:, :, None]
    scores = jnp.where(visible, scores, floor_value)
    maximum = jnp.max(scores, axis=2)
    weights = jnp.where(visible, jnp.exp(scores - maximum[:, :, None]), 0.0)
    weight_sum = jnp.sum(weights, axis=2)
    blended = jnp.einsum(
        "rqk,rkv->rqv",
        weights.astype(jnp.bfloat16),
        suffix[:, :, :KVR],
        preferred_element_type=jnp.float32,
    )
    flat_rows = queries_own.shape[0] * queries_own.shape[1]
    return (
        maximum.reshape(flat_rows),
        weight_sum.reshape(flat_rows),
        blended.reshape(flat_rows, KVR),
    )


def combine(first, second):
    maximum = jnp.maximum(first[0], second[0])
    scale_first = jnp.exp(first[0] - maximum)
    scale_second = jnp.exp(second[0] - maximum)
    weight_sum = first[1] * scale_first + second[1] * scale_second
    blended = first[2] * scale_first[:, None] + second[2] * scale_second[:, None]
    return (maximum, weight_sum, blended)


def per_device(queries, prefix_kv, suffix_kv, lengths):
    request_count, query_rows, latent_width = queries.shape
    first_key = lax.axis_index("row") * suffix_kv.shape[1]
    softmax_state = suffix_state(queries, suffix_kv, lengths, first_key)
    query_flat = queries.reshape(request_count * query_rows, latent_width)
    softmax_state = sweeper(
        query_flat, softmax_state, lax.all_gather(prefix_kv, "col", axis=0, tiled=True)
    )
    maximum, weight_sum, blended = merged(softmax_state, "row", combine)
    return (
        (blended / weight_sum[:, None]).astype(jnp.bfloat16).reshape(request_count, query_rows, KVR)
    )


END_FIRST = [("near", (0, 0, 0)), ("x", (0, 0, 0)), ("near", (0, 0, 1)), ("x", (0, 0, 1))]
END_EVENTS = [
    ((0, 1, 0), ["x"]),
    ((1, 0, 0), []),
    ((0, 1, 1), []),
    ((1, 0, 1), ["near"]),
    ((0, 2, 0), ["x"]),
    ((1, 1, 0), []),
    ((0, 2, 1), ["x"]),
    ((1, 2, 0), []),
    ((0, 3, 0), ["x"]),
    ((1, 2, 1), []),
    ((0, 3, 1), ["x"]),
    ((1, 3, 0), []),
    ((1, 1, 1), []),
    ((1, 3, 1), []),
]
MID_FIRST = [
    ("near", (0, 1, 0)), ("up", (0, 1, 0)), ("x", (0, 1, 1)),
    ("near", (0, 1, 1)), ("up", (0, 1, 1)), ("x", (0, 1, 0)),
]
MID_EVENTS = [
    ((0, 2, 0), ["near", "x"]),
    ((0, 0, 0), ["up", "x"]),
    ((1, 1, 1), []),
    ((0, 2, 1), ["near"]),
    ((0, 0, 1), ["up", ("up", (1, 1, 1))]),
    ((1, 1, 0), []),
    ((0, 3, 0), ["near", "x"]),
    ((1, 0, 1), []),
    ((1, 0, 0), []),
    ((0, 3, 1), ["near", "x", ("near", (1, 1, 1))]),
    ((1, 2, 0), []),
    ((1, 2, 1), []),
    ((1, 3, 0), []),
    ((1, 3, 1), []),
]
CHUNK = 256
LOG2E = 1.4426950408889634


def dot_t(a, b):
    return lax.dot_general(a, b, (((1,), (1,)), ((), ())), preferred_element_type=jnp.float32)


def gather_attend(
    q_hbm, prefix_hbm, suffix_hbm, lengths, out_hbm,
    q_flipped, q, keys, suffix, result, top, total, acc,
    local_sem, x_send, near_send, up_send, sib_send, recv, sib_recv, suf_send, suf_recv, out_send, out_recv,
):
    group, row, col = lax.axis_index("group"), lax.axis_index("row"), lax.axis_index("col")
    z, x = col // 2, col % 2
    flip = z // 2
    place = z + flip * (3 - 2 * z)
    at_end = place == 0
    unit = prefix_hbm.shape[1] // 2
    half_suffix = suffix_hbm.shape[2]
    other = 1 - row

    def line(p):
        return p + flip * (3 - 2 * p)

    def index(name):
        other_x, p, h = name
        return ((x + other_x - 2 * x * other_x) * 4 + line(p)) * 2 + h

    def slot(u, r):
        return keys.at[u, r]

    devices = {
        "x": (group, row, z * 2 + 1 - x),
        "end_near": (group, row, line(1) * 2 + x),
        "mid_near": (group, row, line(0) * 2 + x),
        "up": (group, row, line(2) * 2 + x),
    }
    sibling = (group, other, col)

    def remote(src, dst, send_sem, recv_sem, device):
        return pltpu.make_async_remote_copy(
            src_ref=src, dst_ref=dst, send_sem=send_sem, recv_sem=recv_sem,
            device_id=device, device_id_type=pl.DeviceIdType.MESH,
        )

    barrier = pltpu.get_barrier_semaphore()

    def greet(device):
        pl.semaphore_signal(barrier, inc=1, device_id=device, device_id_type=pl.DeviceIdType.MESH)

    greet(sibling)
    greet(devices["x"])

    q_in = pltpu.make_async_copy(q_hbm.at[row], q_flipped, local_sem.at[0])
    q_in.start()
    own_in = []
    for h in range(2):
        own_in.append(
            pltpu.make_async_copy(
                prefix_hbm.at[:, pl.ds(h * unit, unit)], slot(index_own(col, h, z, x), row), local_sem.at[1 + h]
            )
        )
        own_in[-1].start()
    suffix_in = pltpu.make_async_copy(suffix_hbm.at[row], suffix.at[row], local_sem.at[3])
    suffix_in.start()

    @pl.when(at_end)
    def _():
        greet(devices["end_near"])
        pl.semaphore_wait(barrier, 3)

    @pl.when(jnp.logical_not(at_end))
    def _():
        greet(devices["mid_near"])
        greet(devices["up"])
        pl.semaphore_wait(barrier, 4)

    sems = {"x": x_send, "near": near_send, "up": up_send}

    def make_send(kind, counts, link, name, from_hbm):
        at = counts[link]
        counts[link] += 1
        where = (kind + "_near") if link == "near" else link

        def build():
            u = index(name)
            src = prefix_hbm.at[:, pl.ds(name[2] * unit, unit)] if from_hbm else slot(u, row)
            return remote(src, slot(u, row), sems[link].at[at], recv.at[u], devices[where])

        return build

    def plan(kind, first, events):
        counts = {"x": 0, "near": 0, "up": 0}
        opening = [make_send(kind, counts, link, name, True) for link, name in first]
        after = []
        for name, links in events:
            sends = []
            for link in links:
                if isinstance(link, tuple):
                    sends.append(make_send(kind, counts, link[0], link[1], False))
                else:
                    sends.append(make_send(kind, counts, link, name, False))
            after.append(sends)
        return opening, after

    end_opening, end_after = plan("end", END_FIRST, END_EVENTS)
    mid_opening, mid_after = plan("mid", MID_FIRST, MID_EVENTS)

    def both(end_list, mid_list, act):
        if end_list:
            @pl.when(at_end)
            def _():
                for build in end_list:
                    act(build())
        if mid_list:
            @pl.when(jnp.logical_not(at_end))
            def _():
                for build in mid_list:
                    act(build())

    both(end_opening, mid_opening, lambda copy: copy.start())

    sib_sends = []
    own_units = [index_own(col, h, z, x) for h in range(2)]
    for h in range(2):
        copy = remote(
            prefix_hbm.at[:, pl.ds(h * unit, unit)], slot(own_units[h], row),
            sib_send.at[h], sib_recv.at[own_units[h]], sibling,
        )
        copy.start()
        sib_sends.append(copy)
    suffix_out = remote(suffix_hbm.at[other], suffix.at[row], suf_send, suf_recv, sibling)
    suffix_out.start()

    scale = softmax_scale * LOG2E
    top[...] = jnp.full(top.shape, floor_value, jnp.float32)
    total[...] = jnp.zeros(total.shape, jnp.float32)
    acc[...] = jnp.zeros(acc.shape, jnp.float32)
    length = lengths[row]

    def attend(block, first_key=None):
        scores = jnp.dot(q[...], block, preferred_element_type=jnp.float32) * scale
        if first_key is not None:
            shape = scores.shape
            key = first_key + lax.broadcasted_iota(jnp.int32, shape, 1)
            position = lax.broadcasted_iota(jnp.int32, shape, 0) // H
            scores = jnp.where(key < length - POS + 1 + position, scores, floor_value)
        before = top[...]
        now = jnp.maximum(before, jnp.max(scores, axis=1, keepdims=True))
        weights = jnp.exp2(scores - now)
        rescale = jnp.exp2(before - now)
        top[...] = now
        total[...] = total[...] * rescale + jnp.sum(weights, axis=1, keepdims=True)
        acc[...] = acc[...] * rescale + dot_t(weights.astype(jnp.bfloat16), block[:KVR, :])

    def attend_unit(u):
        attend(jnp.concatenate([keys[u, 0], keys[u, 1]], axis=1))

    def await_sibling(u):
        remote(slot(u, row), slot(u, other), sib_send.at[0], sib_recv.at[u], sibling).wait_recv()

    pieces = half_suffix // CHUNK

    def attend_suffix(i):
        if i == 0:
            suffix_in.wait()
        if i == pieces:
            remote(suffix.at[row], suffix.at[other], suf_send, suf_recv, sibling).wait_recv()
        part = row if i < pieces else other
        start = (i % pieces) * CHUNK
        attend(suffix[part, :, start : start + CHUNK], part * half_suffix + start)

    q_in.wait()
    q[...] = q_flipped[...].T
    for h in range(2):
        own_in[h].wait()
    for u in own_units:
        await_sibling(u)
        attend_unit(u)

    steps = len(END_EVENTS)
    names = []
    for k in range(steps):
        u = jnp.where(at_end, index(END_EVENTS[k][0]), index(MID_EVENTS[k][0]))
        remote(slot(u, row), slot(u, row), sib_send.at[0], recv.at[u], sibling).wait_recv()
        both(end_after[k], mid_after[k], lambda copy: copy.start())
        copy = remote(slot(u, row), slot(u, row), sib_send.at[2 + k], sib_recv.at[u], sibling)
        copy.start()
        sib_sends.append(copy)
        names.append(u)
        if k < 2 * pieces:
            attend_suffix(k)
        if k >= 1:
            await_sibling(names[k - 1])
            attend_unit(names[k - 1])
    for i in range(steps, 2 * pieces):
        attend_suffix(i)
    await_sibling(names[-1])
    attend_unit(names[-1])

    result[...] = (acc[...] / total[...]).astype(jnp.bfloat16)
    final = remote(result, out_hbm.at[row], out_send, out_recv, sibling)
    final.start()
    keep = pltpu.make_async_copy(result, out_hbm.at[row], local_sem.at[4])
    keep.start()
    both(
        end_opening + [b for sends in end_after for b in sends],
        mid_opening + [b for sends in mid_after for b in sends],
        lambda copy: copy.wait_send(),
    )
    for copy in sib_sends:
        copy.wait_send()
    suffix_out.wait_send()
    keep.wait()
    final.wait_send()
    remote(result, out_hbm.at[other], out_send, out_recv, sibling).wait_recv()


def index_own(col, h, z, x):
    return (x * 4 + z) * 2 + h


def ring_device(queries, prefix_kv, suffix_kv, lengths):
    requests, query_rows, width = queries.shape
    unit = prefix_kv.shape[0] // 2
    half_suffix = suffix_kv.shape[1]
    dma = pltpu.SemaphoreType.DMA
    anywhere = pl.BlockSpec(memory_space=pl.ANY)
    return pl.pallas_call(
        gather_attend,
        out_shape=jax.ShapeDtypeStruct((requests, query_rows, KVR), jnp.bfloat16),
        in_specs=[anywhere, anywhere, anywhere, pl.BlockSpec(memory_space=pltpu.SMEM)],
        out_specs=anywhere,
        scratch_shapes=[
            pltpu.VMEM((width, query_rows), jnp.bfloat16),
            pltpu.VMEM((query_rows, width), jnp.bfloat16),
            pltpu.VMEM((16, 2, width, unit), jnp.bfloat16),
            pltpu.VMEM((2, width, half_suffix), jnp.bfloat16),
            pltpu.VMEM((query_rows, KVR), jnp.bfloat16),
            pltpu.VMEM((query_rows, 1), jnp.float32),
            pltpu.VMEM((query_rows, 1), jnp.float32),
            pltpu.VMEM((query_rows, KVR), jnp.float32),
            dma((5,)), dma((7,)), dma((7,)), dma((5,)), dma((16,)), dma((16,)), dma((16,)),
            dma, dma, dma, dma,
        ],
        compiler_params=pltpu.CompilerParams(
            collective_id=0, has_side_effects=True, vmem_limit_bytes=56 * 1024 * 1024
        ),
    )(jnp.swapaxes(queries, 1, 2), prefix_kv.T, jnp.swapaxes(suffix_kv, 1, 2), lengths)


def solution(mesh):
    small = dict(mesh.shape) == {"group": 2, "row": 2, "col": 8}
    return jax.shard_map(
        ring_device if small else per_device,
        mesh=mesh,
        in_specs=(
            P(("group", "col"), None, None),
            P(("group", "row", "col"), None),
            P(("group", "col"), "row", None),
            P(("group", "col")),
        ),
        out_specs=P(("group", "col"), None, None),
        check_vma=False,
    )
```

```python
import math

import jax
import jax.numpy as jnp
from jax import lax
from jax.experimental import pallas as pl
from jax.experimental.pallas import tpu as pltpu
from jax.sharding import PartitionSpec as P

H = 128
KVR = 512
POS = 2


softmax_scale = 192.0 ** (-0.5)
floor_value = -1e30


def merged(value, axis, join):
    pieces = jax.tree.map(lambda part: lax.all_gather(part, axis), value)
    head = jax.tree.map(lambda part: part[0], pieces)
    tail = jax.tree.map(lambda part: part[1:], pieces)
    subtotal, _ = lax.scan(lambda subtotal, share: (join(subtotal, share), None), head, tail)
    return subtotal


def absorb(running, query_flat, key_block):
    maximum, weight_sum, blended = running
    scores = (
        jnp.einsum("ml,kl->mk", query_flat, key_block, preferred_element_type=jnp.float32)
        * softmax_scale
    )
    new_max = jnp.maximum(maximum, jnp.max(scores, axis=1))
    weights = jnp.exp(scores - new_max[:, None])
    rescale = jnp.exp(maximum - new_max)
    weight_sum = weight_sum * rescale + jnp.sum(weights, axis=1)
    blended = blended * rescale[:, None] + jnp.dot(
        weights.astype(jnp.bfloat16), key_block[:, :KVR], preferred_element_type=jnp.float32
    )
    return (new_max, weight_sum, blended)


def sweeper(query_flat, running, key_piece):
    key_count = key_piece.shape[0]
    block_size = math.gcd(key_count, 512)
    pieces = key_piece.reshape(key_count // block_size, block_size, key_piece.shape[1])

    def scan_step(carried, key_block):
        return (absorb(carried, query_flat, key_block), None)

    return lax.scan(scan_step, running, pieces)[0]


def suffix_state(queries_own, suffix, lengths, first_key):
    scores = (
        jnp.einsum("rql,rkl->rqk", queries_own, suffix, preferred_element_type=jnp.float32)
        * softmax_scale
    )
    key_index = first_key + jnp.arange(suffix.shape[1], dtype=jnp.int32)
    position = jnp.arange(queries_own.shape[1], dtype=jnp.int32) // H
    key_limit = lengths[:, None] - POS + 1 + position[None, :]
    visible = key_index[None, None, :] < key_limit[:, :, None]
    scores = jnp.where(visible, scores, floor_value)
    maximum = jnp.max(scores, axis=2)
    weights = jnp.where(visible, jnp.exp(scores - maximum[:, :, None]), 0.0)
    weight_sum = jnp.sum(weights, axis=2)
    blended = jnp.einsum(
        "rqk,rkv->rqv",
        weights.astype(jnp.bfloat16),
        suffix[:, :, :KVR],
        preferred_element_type=jnp.float32,
    )
    flat_rows = queries_own.shape[0] * queries_own.shape[1]
    return (
        maximum.reshape(flat_rows),
        weight_sum.reshape(flat_rows),
        blended.reshape(flat_rows, KVR),
    )


def combine(first, second):
    maximum = jnp.maximum(first[0], second[0])
    scale_first = jnp.exp(first[0] - maximum)
    scale_second = jnp.exp(second[0] - maximum)
    weight_sum = first[1] * scale_first + second[1] * scale_second
    blended = first[2] * scale_first[:, None] + second[2] * scale_second[:, None]
    return (maximum, weight_sum, blended)


def per_device(queries, prefix_kv, suffix_kv, lengths):
    request_count, query_rows, latent_width = queries.shape
    first_key = lax.axis_index("row") * suffix_kv.shape[1]
    softmax_state = suffix_state(queries, suffix_kv, lengths, first_key)
    query_flat = queries.reshape(request_count * query_rows, latent_width)
    softmax_state = sweeper(
        query_flat, softmax_state, lax.all_gather(prefix_kv, "col", axis=0, tiled=True)
    )
    maximum, weight_sum, blended = merged(softmax_state, "row", combine)
    return (
        (blended / weight_sum[:, None]).astype(jnp.bfloat16).reshape(request_count, query_rows, KVR)
    )


END_FIRST = [("near", (0, 0, 0)), ("x", (0, 0, 0)), ("near", (0, 0, 1)), ("x", (0, 0, 1))]
END_EVENTS = [
    ((0, 1, 0), ["x"]),
    ((1, 0, 0), []),
    ((0, 1, 1), []),
    ((1, 0, 1), ["near"]),
    ((0, 2, 0), ["x"]),
    ((1, 1, 0), []),
    ((0, 2, 1), ["x"]),
    ((1, 2, 0), []),
    ((0, 3, 0), ["x"]),
    ((1, 2, 1), []),
    ((0, 3, 1), ["x"]),
    ((1, 3, 0), []),
    ((1, 1, 1), []),
    ((1, 3, 1), []),
]
MID_FIRST = [
    ("near", (0, 1, 0)), ("up", (0, 1, 0)), ("x", (0, 1, 1)),
    ("near", (0, 1, 1)), ("up", (0, 1, 1)), ("x", (0, 1, 0)),
]
MID_EVENTS = [
    ((0, 2, 0), ["near", "x"]),
    ((0, 0, 0), ["up", "x"]),
    ((1, 1, 1), []),
    ((0, 2, 1), ["near"]),
    ((0, 0, 1), ["up", ("up", (1, 1, 1))]),
    ((1, 1, 0), []),
    ((0, 3, 0), ["near", "x"]),
    ((1, 0, 1), []),
    ((1, 0, 0), []),
    ((0, 3, 1), ["near", "x", ("near", (1, 1, 1))]),
    ((1, 2, 0), []),
    ((1, 2, 1), []),
    ((1, 3, 0), []),
    ((1, 3, 1), []),
]
END_GROUPS = [2] * 7
MID_GROUPS = [3, 3, 3, 2, 2, 1]
PARTS = 2
CHUNK = 256
LOG2E = 1.4426950408889634


def in_parts(events, groups):
    order, start = [], 0
    for size in groups:
        order += [(k, part) for part in range(PARTS) for k in range(start, start + size)]
        start += size
    return order


def dot_t(a, b):
    return lax.dot_general(a, b, (((1,), (1,)), ((), ())), preferred_element_type=jnp.float32)


def gather_attend(
    q_hbm, prefix_hbm, suffix_hbm, lengths, out_hbm,
    q_flipped, q, keys, suffix, result, top, total, acc,
    local_sem, x_send, near_send, up_send, sib_send, recv, sib_recv, suf_send, suf_recv, out_send, out_recv,
):
    group, row, col = lax.axis_index("group"), lax.axis_index("row"), lax.axis_index("col")
    z, x = col // 2, col % 2
    flip = z // 2
    place = z + flip * (3 - 2 * z)
    at_end = place == 0
    unit = prefix_hbm.shape[1] // 2
    half_suffix = suffix_hbm.shape[2]
    other = 1 - row

    def line(p):
        return p + flip * (3 - 2 * p)

    def index(name):
        other_x, p, h = name
        return ((x + other_x - 2 * x * other_x) * 4 + line(p)) * 2 + h

    def slot(u, r):
        return keys.at[u, r]

    devices = {
        "x": (group, row, z * 2 + 1 - x),
        "end_near": (group, row, line(1) * 2 + x),
        "mid_near": (group, row, line(0) * 2 + x),
        "up": (group, row, line(2) * 2 + x),
    }
    sibling = (group, other, col)

    def remote(src, dst, send_sem, recv_sem, device):
        return pltpu.make_async_remote_copy(
            src_ref=src, dst_ref=dst, send_sem=send_sem, recv_sem=recv_sem,
            device_id=device, device_id_type=pl.DeviceIdType.MESH,
        )

    barrier = pltpu.get_barrier_semaphore()

    def greet(device):
        pl.semaphore_signal(barrier, inc=1, device_id=device, device_id_type=pl.DeviceIdType.MESH)

    greet(sibling)
    greet(devices["x"])

    q_in = pltpu.make_async_copy(q_hbm.at[row], q_flipped, local_sem.at[0])
    q_in.start()
    own_in = []
    for h in range(2):
        own_in.append(
            pltpu.make_async_copy(
                prefix_hbm.at[:, pl.ds(h * unit, unit)], slot(index_own(col, h, z, x), row), local_sem.at[1 + h]
            )
        )
        own_in[-1].start()
    suffix_in = pltpu.make_async_copy(suffix_hbm.at[row], suffix.at[row], local_sem.at[3])
    suffix_in.start()

    @pl.when(at_end)
    def _():
        greet(devices["end_near"])
        pl.semaphore_wait(barrier, 3)

    @pl.when(jnp.logical_not(at_end))
    def _():
        greet(devices["mid_near"])
        greet(devices["up"])
        pl.semaphore_wait(barrier, 4)

    sems = {"x": x_send, "near": near_send, "up": up_send}

    span = prefix_hbm.shape[0] // PARTS

    def piece(u, r, part):
        return keys.at[u, r, pl.ds(part * span, span), :]

    def own_piece(h, part):
        return prefix_hbm.at[pl.ds(part * span, span), pl.ds(h * unit, unit)]

    def make_send(kind, counts, link, name, part, from_hbm):
        at = counts[link]
        counts[link] += 1
        where = (kind + "_near") if link == "near" else link

        def build():
            u = index(name)
            src = own_piece(name[2], part) if from_hbm else piece(u, row, part)
            return remote(src, piece(u, row, part), sems[link].at[at], recv.at[u, part], devices[where])

        return build

    def plan(kind, first, events, order):
        counts = {"x": 0, "near": 0, "up": 0}
        opening = [
            make_send(kind, counts, link, name, part, True)
            for at in range(0, len(first), len(first) // 2)
            for part in range(PARTS)
            for link, name in first[at : at + len(first) // 2]
        ]
        after = []
        for k, part in order:
            name, links = events[k]
            pairs = [link if isinstance(link, tuple) else (link, name) for link in links]
            after.append([make_send(kind, counts, link, sent, part, False) for link, sent in pairs])
        return opening, after

    end_order = in_parts(END_EVENTS, END_GROUPS)
    mid_order = in_parts(MID_EVENTS, MID_GROUPS)
    end_opening, end_after = plan("end", END_FIRST, END_EVENTS, end_order)
    mid_opening, mid_after = plan("mid", MID_FIRST, MID_EVENTS, mid_order)

    def both(end_list, mid_list, act):
        if end_list:
            @pl.when(at_end)
            def _():
                for build in end_list:
                    act(build())
        if mid_list:
            @pl.when(jnp.logical_not(at_end))
            def _():
                for build in mid_list:
                    act(build())

    both(end_opening, mid_opening, lambda copy: copy.start())

    sib_sends = []
    own_units = [index_own(col, h, z, x) for h in range(2)]
    for h in range(2):
        copy = remote(
            prefix_hbm.at[:, pl.ds(h * unit, unit)], slot(own_units[h], row),
            sib_send.at[h, 0], sib_recv.at[own_units[h], 0], sibling,
        )
        copy.start()
        sib_sends.append(copy)
    suffix_out = remote(suffix_hbm.at[other], suffix.at[row], suf_send, suf_recv, sibling)
    suffix_out.start()

    scale = softmax_scale * LOG2E
    top[...] = jnp.full(top.shape, floor_value, jnp.float32)
    total[...] = jnp.zeros(total.shape, jnp.float32)
    acc[...] = jnp.zeros(acc.shape, jnp.float32)
    length = lengths[row]

    def attend(block, first_key=None):
        scores = jnp.dot(q[...], block, preferred_element_type=jnp.float32) * scale
        if first_key is not None:
            shape = scores.shape
            key = first_key + lax.broadcasted_iota(jnp.int32, shape, 1)
            position = lax.broadcasted_iota(jnp.int32, shape, 0) // H
            scores = jnp.where(key < length - POS + 1 + position, scores, floor_value)
        before = top[...]
        now = jnp.maximum(before, jnp.max(scores, axis=1, keepdims=True))
        weights = jnp.exp2(scores - now)
        rescale = jnp.exp2(before - now)
        top[...] = now
        total[...] = total[...] * rescale + jnp.sum(weights, axis=1, keepdims=True)
        acc[...] = acc[...] * rescale + dot_t(weights.astype(jnp.bfloat16), block[:KVR, :])

    def attend_unit(u):
        attend(jnp.concatenate([keys[u, 0], keys[u, 1]], axis=1))

    def await_sibling(u, whole=False):
        if whole:
            remote(slot(u, row), slot(u, other), sib_send.at[0, 0], sib_recv.at[u, 0], sibling).wait_recv()
        else:
            for part in range(PARTS):
                remote(
                    piece(u, row, part), piece(u, other, part),
                    sib_send.at[0, part], sib_recv.at[u, part], sibling,
                ).wait_recv()

    pieces = half_suffix // CHUNK

    def attend_suffix(i):
        if i == 0:
            suffix_in.wait()
        if i == pieces:
            remote(suffix.at[row], suffix.at[other], suf_send, suf_recv, sibling).wait_recv()
        part = row if i < pieces else other
        start = (i % pieces) * CHUNK
        attend(suffix[part, :, start : start + CHUNK], part * half_suffix + start)

    q_in.wait()
    q[...] = q_flipped[...].T
    for h in range(2):
        own_in[h].wait()
    for u in own_units:
        await_sibling(u, True)
        attend_unit(u)

    def finished(order):
        return [k for k, part in order if part == PARTS - 1]

    def ready(order):
        return [at for at, (k, part) in enumerate(order) if part == PARTS - 1]

    units = [
        jnp.where(at_end, index(END_EVENTS[a][0]), index(MID_EVENTS[b][0]))
        for a, b in zip(finished(end_order), finished(mid_order))
    ]
    due = [max(a, b) + 1 for a, b in zip(ready(end_order), ready(mid_order))]
    steps = len(end_order)
    done, suffix_done = 0, 0
    for i in range(steps):
        a, b = end_order[i], mid_order[i]
        u = jnp.where(at_end, index(END_EVENTS[a[0]][0]), index(MID_EVENTS[b[0]][0]))
        if a[1] == b[1]:
            part = a[1]
        else:
            part = jnp.where(at_end, a[1], b[1])
        here = (u, row, pl.ds(pl.multiple_of(part * span, 16), span), slice(None))
        remote(keys.at[here], keys.at[here], sib_send.at[0, 0], recv.at[u, part], sibling).wait_recv()
        both(end_after[i], mid_after[i], lambda copy: copy.start())
        copy = remote(
            keys.at[here], keys.at[here], sib_send.at[2 + i // PARTS, i % PARTS], sib_recv.at[u, part], sibling
        )
        copy.start()
        sib_sends.append(copy)
        if i % 2 == 0 and suffix_done < 2 * pieces:
            attend_suffix(suffix_done)
            suffix_done += 1
        while done < len(due) and due[done] <= i:
            await_sibling(units[done])
            attend_unit(units[done])
            done += 1
    for at in range(suffix_done, 2 * pieces):
        attend_suffix(at)
    for at in range(done, len(due)):
        await_sibling(units[at])
        attend_unit(units[at])

    result[...] = (acc[...] / total[...]).astype(jnp.bfloat16)
    final = remote(result, out_hbm.at[row], out_send, out_recv, sibling)
    final.start()
    keep = pltpu.make_async_copy(result, out_hbm.at[row], local_sem.at[4])
    keep.start()
    both(
        end_opening + [b for sends in end_after for b in sends],
        mid_opening + [b for sends in mid_after for b in sends],
        lambda copy: copy.wait_send(),
    )
    for copy in sib_sends:
        copy.wait_send()
    suffix_out.wait_send()
    keep.wait()
    final.wait_send()
    remote(result, out_hbm.at[other], out_send, out_recv, sibling).wait_recv()


def index_own(col, h, z, x):
    return (x * 4 + z) * 2 + h


def ring_device(queries, prefix_kv, suffix_kv, lengths):
    requests, query_rows, width = queries.shape
    unit = prefix_kv.shape[0] // 2
    half_suffix = suffix_kv.shape[1]
    dma = pltpu.SemaphoreType.DMA
    anywhere = pl.BlockSpec(memory_space=pl.ANY)
    return pl.pallas_call(
        gather_attend,
        out_shape=jax.ShapeDtypeStruct((requests, query_rows, KVR), jnp.bfloat16),
        in_specs=[anywhere, anywhere, anywhere, pl.BlockSpec(memory_space=pltpu.SMEM)],
        out_specs=anywhere,
        scratch_shapes=[
            pltpu.VMEM((width, query_rows), jnp.bfloat16),
            pltpu.VMEM((query_rows, width), jnp.bfloat16),
            pltpu.VMEM((16, 2, width, unit), jnp.bfloat16),
            pltpu.VMEM((2, width, half_suffix), jnp.bfloat16),
            pltpu.VMEM((query_rows, KVR), jnp.bfloat16),
            pltpu.VMEM((query_rows, 1), jnp.float32),
            pltpu.VMEM((query_rows, 1), jnp.float32),
            pltpu.VMEM((query_rows, KVR), jnp.float32),
            dma((5,)), dma((7 * PARTS,)), dma((7 * PARTS,)), dma((5 * PARTS,)),
            dma((16, PARTS)), dma((16, PARTS)), dma((16, PARTS)),
            dma, dma, dma, dma,
        ],
        compiler_params=pltpu.CompilerParams(
            collective_id=0, has_side_effects=True, vmem_limit_bytes=57344 * 1024
        ),
    )(jnp.swapaxes(queries, 1, 2), prefix_kv.T, jnp.swapaxes(suffix_kv, 1, 2), lengths)


def solution(mesh):
    small = dict(mesh.shape) == {"group": 2, "row": 2, "col": 8}
    return jax.shard_map(
        ring_device if small else per_device,
        mesh=mesh,
        in_specs=(
            P(("group", "col"), None, None),
            P(("group", "row", "col"), None),
            P(("group", "col"), "row", None),
            P(("group", "col")),
        ),
        out_specs=P(("group", "col"), None, None),
        check_vma=False,
    )
```

```python
import math

import jax
import jax.numpy as jnp
from jax import lax
from jax.experimental import pallas as pl
from jax.experimental.pallas import tpu as pltpu
from jax.sharding import PartitionSpec as P

H = 128
KVR = 512
POS = 2


softmax_scale = 192.0 ** (-0.5)
floor_value = -1e30


def merged(value, axis, join):
    pieces = jax.tree.map(lambda part: lax.all_gather(part, axis), value)
    head = jax.tree.map(lambda part: part[0], pieces)
    tail = jax.tree.map(lambda part: part[1:], pieces)
    subtotal, _ = lax.scan(lambda subtotal, share: (join(subtotal, share), None), head, tail)
    return subtotal


def absorb(running, query_flat, key_block):
    maximum, weight_sum, blended = running
    scores = (
        jnp.einsum("ml,kl->mk", query_flat, key_block, preferred_element_type=jnp.float32)
        * softmax_scale
    )
    new_max = jnp.maximum(maximum, jnp.max(scores, axis=1))
    weights = jnp.exp(scores - new_max[:, None])
    rescale = jnp.exp(maximum - new_max)
    weight_sum = weight_sum * rescale + jnp.sum(weights, axis=1)
    blended = blended * rescale[:, None] + jnp.dot(
        weights.astype(jnp.bfloat16), key_block[:, :KVR], preferred_element_type=jnp.float32
    )
    return (new_max, weight_sum, blended)


def sweeper(query_flat, running, key_piece):
    key_count = key_piece.shape[0]
    block_size = math.gcd(key_count, 512)
    pieces = key_piece.reshape(key_count // block_size, block_size, key_piece.shape[1])

    def scan_step(carried, key_block):
        return (absorb(carried, query_flat, key_block), None)

    return lax.scan(scan_step, running, pieces)[0]


def suffix_state(queries_own, suffix, lengths, first_key):
    scores = (
        jnp.einsum("rql,rkl->rqk", queries_own, suffix, preferred_element_type=jnp.float32)
        * softmax_scale
    )
    key_index = first_key + jnp.arange(suffix.shape[1], dtype=jnp.int32)
    position = jnp.arange(queries_own.shape[1], dtype=jnp.int32) // H
    key_limit = lengths[:, None] - POS + 1 + position[None, :]
    visible = key_index[None, None, :] < key_limit[:, :, None]
    scores = jnp.where(visible, scores, floor_value)
    maximum = jnp.max(scores, axis=2)
    weights = jnp.where(visible, jnp.exp(scores - maximum[:, :, None]), 0.0)
    weight_sum = jnp.sum(weights, axis=2)
    blended = jnp.einsum(
        "rqk,rkv->rqv",
        weights.astype(jnp.bfloat16),
        suffix[:, :, :KVR],
        preferred_element_type=jnp.float32,
    )
    flat_rows = queries_own.shape[0] * queries_own.shape[1]
    return (
        maximum.reshape(flat_rows),
        weight_sum.reshape(flat_rows),
        blended.reshape(flat_rows, KVR),
    )


def combine(first, second):
    maximum = jnp.maximum(first[0], second[0])
    scale_first = jnp.exp(first[0] - maximum)
    scale_second = jnp.exp(second[0] - maximum)
    weight_sum = first[1] * scale_first + second[1] * scale_second
    blended = first[2] * scale_first[:, None] + second[2] * scale_second[:, None]
    return (maximum, weight_sum, blended)


def per_device(queries, prefix_kv, suffix_kv, lengths):
    request_count, query_rows, latent_width = queries.shape
    first_key = lax.axis_index("row") * suffix_kv.shape[1]
    softmax_state = suffix_state(queries, suffix_kv, lengths, first_key)
    query_flat = queries.reshape(request_count * query_rows, latent_width)
    softmax_state = sweeper(
        query_flat, softmax_state, lax.all_gather(prefix_kv, "col", axis=0, tiled=True)
    )
    maximum, weight_sum, blended = merged(softmax_state, "row", combine)
    return (
        (blended / weight_sum[:, None]).astype(jnp.bfloat16).reshape(request_count, query_rows, KVR)
    )


END_FIRST = [("near", (0, 0, 0)), ("x", (0, 0, 0)), ("near", (0, 0, 1)), ("x", (0, 0, 1))]
END_EVENTS = [
    ((0, 1, 0), ["x"]),
    ((1, 0, 0), []),
    ((0, 1, 1), []),
    ((1, 0, 1), ["near"]),
    ((0, 2, 0), ["x"]),
    ((1, 1, 0), []),
    ((0, 2, 1), ["x"]),
    ((1, 2, 0), []),
    ((0, 3, 0), ["x"]),
    ((1, 2, 1), []),
    ((0, 3, 1), ["x"]),
    ((1, 3, 0), []),
    ((1, 1, 1), []),
    ((1, 3, 1), []),
]
MID_FIRST = [
    ("near", (0, 1, 0)), ("up", (0, 1, 0)), ("x", (0, 1, 1)),
    ("near", (0, 1, 1)), ("up", (0, 1, 1)), ("x", (0, 1, 0)),
]
MID_EVENTS = [
    ((0, 2, 0), ["near", "x"]),
    ((0, 0, 0), ["up", "x"]),
    ((1, 1, 1), []),
    ((0, 2, 1), ["near"]),
    ((0, 0, 1), ["up", ("up", (1, 1, 1))]),
    ((1, 1, 0), []),
    ((0, 3, 0), ["near", "x"]),
    ((1, 0, 1), []),
    ((1, 0, 0), []),
    ((0, 3, 1), ["near", "x", ("near", (1, 1, 1))]),
    ((1, 2, 0), []),
    ((1, 2, 1), []),
    ((1, 3, 0), []),
    ((1, 3, 1), []),
]
CHUNK = 256
LOG2E = 1.4426950408889634


def dot_t(a, b):
    return lax.dot_general(a, b, (((1,), (1,)), ((), ())), preferred_element_type=jnp.float32)


def gather_attend(
    q_hbm, prefix_hbm, suffix_hbm, lengths, out_hbm,
    q_flipped, q, keys, suffix, result, top, total, acc,
    local_sem, x_send, near_send, up_send, sib_send, recv, sib_recv, suf_send, suf_recv, out_send, out_recv,
):
    group, row, col = lax.axis_index("group"), lax.axis_index("row"), lax.axis_index("col")
    z, x = col // 2, col % 2
    flip = z // 2
    place = z + flip * (3 - 2 * z)
    at_end = place == 0
    unit = prefix_hbm.shape[1] // 2
    half_suffix = suffix_hbm.shape[2]
    other = 1 - row

    def line(p):
        return p + flip * (3 - 2 * p)

    def index(name):
        other_x, p, h = name
        return ((x + other_x - 2 * x * other_x) * 4 + line(p)) * 2 + h

    def slot(u, r):
        return keys.at[u, r]

    devices = {
        "x": (group, row, z * 2 + 1 - x),
        "end_near": (group, row, line(1) * 2 + x),
        "mid_near": (group, row, line(0) * 2 + x),
        "up": (group, row, line(2) * 2 + x),
    }
    sibling = (group, other, col)

    def remote(src, dst, send_sem, recv_sem, device):
        return pltpu.make_async_remote_copy(
            src_ref=src, dst_ref=dst, send_sem=send_sem, recv_sem=recv_sem,
            device_id=device, device_id_type=pl.DeviceIdType.MESH,
        )

    barrier = pltpu.get_barrier_semaphore()

    def greet(device):
        pl.semaphore_signal(barrier, inc=1, device_id=device, device_id_type=pl.DeviceIdType.MESH)

    greet(sibling)
    greet(devices["x"])

    q_in = pltpu.make_async_copy(q_hbm.at[row], q_flipped, local_sem.at[0])
    q_in.start()
    own_in = []
    for h in range(2):
        own_in.append(
            pltpu.make_async_copy(
                prefix_hbm.at[:, pl.ds(h * unit, unit)], slot(index_own(col, h, z, x), row), local_sem.at[1 + h]
            )
        )
        own_in[-1].start()
    suffix_in = pltpu.make_async_copy(suffix_hbm.at[row], suffix.at[row], local_sem.at[3])
    suffix_in.start()

    @pl.when(at_end)
    def _():
        greet(devices["end_near"])
        pl.semaphore_wait(barrier, 3)

    @pl.when(jnp.logical_not(at_end))
    def _():
        greet(devices["mid_near"])
        greet(devices["up"])
        pl.semaphore_wait(barrier, 4)

    sems = {"x": x_send, "near": near_send, "up": up_send}

    def make_send(kind, counts, link, name, from_hbm):
        at = counts[link]
        counts[link] += 1
        where = (kind + "_near") if link == "near" else link

        def build():
            u = index(name)
            src = prefix_hbm.at[:, pl.ds(name[2] * unit, unit)] if from_hbm else slot(u, row)
            return remote(src, slot(u, row), sems[link].at[at], recv.at[u], devices[where])

        return build

    def plan(kind, first, events):
        counts = {"x": 0, "near": 0, "up": 0}
        opening = [make_send(kind, counts, link, name, True) for link, name in first]
        after = []
        for name, links in events:
            sends = []
            for link in links:
                if isinstance(link, tuple):
                    sends.append(make_send(kind, counts, link[0], link[1], False))
                else:
                    sends.append(make_send(kind, counts, link, name, False))
            after.append(sends)
        return opening, after

    end_opening, end_after = plan("end", END_FIRST, END_EVENTS)
    mid_opening, mid_after = plan("mid", MID_FIRST, MID_EVENTS)

    def both(end_list, mid_list, act):
        if end_list:
            @pl.when(at_end)
            def _():
                for build in end_list:
                    act(build())
        if mid_list:
            @pl.when(jnp.logical_not(at_end))
            def _():
                for build in mid_list:
                    act(build())

    both(end_opening, mid_opening, lambda copy: copy.start())

    sib_sends = []
    own_units = [index_own(col, h, z, x) for h in range(2)]
    for h in range(2):
        copy = remote(
            prefix_hbm.at[:, pl.ds(h * unit, unit)], slot(own_units[h], row),
            sib_send.at[h], sib_recv.at[own_units[h]], sibling,
        )
        copy.start()
        sib_sends.append(copy)
    suffix_out = remote(suffix_hbm.at[other], suffix.at[row], suf_send, suf_recv, sibling)
    suffix_out.start()

    scale = softmax_scale * LOG2E
    top[...] = jnp.full(top.shape, floor_value, jnp.float32)
    total[...] = jnp.zeros(total.shape, jnp.float32)
    acc[...] = jnp.zeros(acc.shape, jnp.float32)
    length = lengths[row]

    def attend(block, first_key=None):
        scores = jnp.dot(q[...], block, preferred_element_type=jnp.float32) * scale
        if first_key is not None:
            shape = scores.shape
            key = first_key + lax.broadcasted_iota(jnp.int32, shape, 1)
            position = lax.broadcasted_iota(jnp.int32, shape, 0) // H
            scores = jnp.where(key < length - POS + 1 + position, scores, floor_value)
        before = top[...]
        now = jnp.maximum(before, jnp.max(scores, axis=1, keepdims=True))
        weights = jnp.exp2(scores - now)
        rescale = jnp.exp2(before - now)
        top[...] = now
        total[...] = total[...] * rescale + jnp.sum(weights, axis=1, keepdims=True)
        acc[...] = acc[...] * rescale + dot_t(weights.astype(jnp.bfloat16), block[:KVR, :])

    def attend_unit(u):
        attend(jnp.concatenate([keys[u, 0], keys[u, 1]], axis=1))

    def await_sibling(u):
        remote(slot(u, row), slot(u, other), sib_send.at[0], sib_recv.at[u], sibling).wait_recv()

    pieces = half_suffix // CHUNK

    def attend_suffix(i):
        if i == 0:
            suffix_in.wait()
        if i == pieces:
            remote(suffix.at[row], suffix.at[other], suf_send, suf_recv, sibling).wait_recv()
        part = row if i < pieces else other
        start = (i % pieces) * CHUNK
        attend(suffix[part, :, start : start + CHUNK], part * half_suffix + start)

    q_in.wait()
    q[...] = q_flipped[...].T
    for h in range(2):
        own_in[h].wait()
    for u in own_units:
        await_sibling(u)
        attend_unit(u)

    for i in range(4):
        attend_suffix(i)
    steps = len(END_EVENTS)
    names = []
    for k in range(steps):
        u = jnp.where(at_end, index(END_EVENTS[k][0]), index(MID_EVENTS[k][0]))
        remote(slot(u, row), slot(u, row), sib_send.at[0], recv.at[u], sibling).wait_recv()
        both(end_after[k], mid_after[k], lambda copy: copy.start())
        copy = remote(slot(u, row), slot(u, row), sib_send.at[2 + k], sib_recv.at[u], sibling)
        copy.start()
        sib_sends.append(copy)
        names.append(u)
        if k >= 4 and k < 12 - 4:
            attend_suffix(k - 4 + 4)
        if k >= 1:
            await_sibling(names[k - 1])
            attend_unit(names[k - 1])
    for i in range(steps, 2 * pieces):
        attend_suffix(i)
    await_sibling(names[-1])
    attend_unit(names[-1])

    result[...] = (acc[...] / total[...]).astype(jnp.bfloat16)
    final = remote(result, out_hbm.at[row], out_send, out_recv, sibling)
    final.start()
    keep = pltpu.make_async_copy(result, out_hbm.at[row], local_sem.at[4])
    keep.start()
    both(
        end_opening + [b for sends in end_after for b in sends],
        mid_opening + [b for sends in mid_after for b in sends],
        lambda copy: copy.wait_send(),
    )
    for copy in sib_sends:
        copy.wait_send()
    suffix_out.wait_send()
    keep.wait()
    final.wait_send()
    remote(result, out_hbm.at[other], out_send, out_recv, sibling).wait_recv()


def index_own(col, h, z, x):
    return (x * 4 + z) * 2 + h


def ring_device(queries, prefix_kv, suffix_kv, lengths):
    requests, query_rows, width = queries.shape
    unit = prefix_kv.shape[0] // 2
    half_suffix = suffix_kv.shape[1]
    dma = pltpu.SemaphoreType.DMA
    anywhere = pl.BlockSpec(memory_space=pl.ANY)
    return pl.pallas_call(
        gather_attend,
        out_shape=jax.ShapeDtypeStruct((requests, query_rows, KVR), jnp.bfloat16),
        in_specs=[anywhere, anywhere, anywhere, pl.BlockSpec(memory_space=pltpu.SMEM)],
        out_specs=anywhere,
        scratch_shapes=[
            pltpu.VMEM((width, query_rows), jnp.bfloat16),
            pltpu.VMEM((query_rows, width), jnp.bfloat16),
            pltpu.VMEM((16, 2, width, unit), jnp.bfloat16),
            pltpu.VMEM((2, width, half_suffix), jnp.bfloat16),
            pltpu.VMEM((query_rows, KVR), jnp.bfloat16),
            pltpu.VMEM((query_rows, 1), jnp.float32),
            pltpu.VMEM((query_rows, 1), jnp.float32),
            pltpu.VMEM((query_rows, KVR), jnp.float32),
            dma((5,)), dma((7,)), dma((7,)), dma((5,)), dma((16,)), dma((16,)), dma((16,)),
            dma, dma, dma, dma,
        ],
        compiler_params=pltpu.CompilerParams(
            collective_id=0, has_side_effects=True, vmem_limit_bytes=56 * 1024 * 1024
        ),
    )(jnp.swapaxes(queries, 1, 2), prefix_kv.T, jnp.swapaxes(suffix_kv, 1, 2), lengths)


def solution(mesh):
    small = dict(mesh.shape) == {"group": 2, "row": 2, "col": 8}
    return jax.shard_map(
        ring_device if small else per_device,
        mesh=mesh,
        in_specs=(
            P(("group", "col"), None, None),
            P(("group", "row", "col"), None),
            P(("group", "col"), "row", None),
            P(("group", "col")),
        ),
        out_specs=P(("group", "col"), None, None),
        check_vma=False,
    )
```

```python
import math

import jax
import jax.numpy as jnp
from jax import lax
from jax.experimental import pallas as pl
from jax.experimental.pallas import tpu as pltpu
from jax.sharding import PartitionSpec as P

H = 128
KVR = 512
POS = 2


softmax_scale = 192.0 ** (-0.5)
floor_value = -1e30


def merged(value, axis, join):
    pieces = jax.tree.map(lambda part: lax.all_gather(part, axis), value)
    head = jax.tree.map(lambda part: part[0], pieces)
    tail = jax.tree.map(lambda part: part[1:], pieces)
    subtotal, _ = lax.scan(lambda subtotal, share: (join(subtotal, share), None), head, tail)
    return subtotal


def absorb(running, query_flat, key_block):
    maximum, weight_sum, blended = running
    scores = (
        jnp.einsum("ml,kl->mk", query_flat, key_block, preferred_element_type=jnp.float32)
        * softmax_scale
    )
    new_max = jnp.maximum(maximum, jnp.max(scores, axis=1))
    weights = jnp.exp(scores - new_max[:, None])
    rescale = jnp.exp(maximum - new_max)
    weight_sum = weight_sum * rescale + jnp.sum(weights, axis=1)
    blended = blended * rescale[:, None] + jnp.dot(
        weights.astype(jnp.bfloat16), key_block[:, :KVR], preferred_element_type=jnp.float32
    )
    return (new_max, weight_sum, blended)


def sweeper(query_flat, running, key_piece):
    key_count = key_piece.shape[0]
    block_size = math.gcd(key_count, 512)
    pieces = key_piece.reshape(key_count // block_size, block_size, key_piece.shape[1])

    def scan_step(carried, key_block):
        return (absorb(carried, query_flat, key_block), None)

    return lax.scan(scan_step, running, pieces)[0]


def suffix_state(queries_own, suffix, lengths, first_key):
    scores = (
        jnp.einsum("rql,rkl->rqk", queries_own, suffix, preferred_element_type=jnp.float32)
        * softmax_scale
    )
    key_index = first_key + jnp.arange(suffix.shape[1], dtype=jnp.int32)
    position = jnp.arange(queries_own.shape[1], dtype=jnp.int32) // H
    key_limit = lengths[:, None] - POS + 1 + position[None, :]
    visible = key_index[None, None, :] < key_limit[:, :, None]
    scores = jnp.where(visible, scores, floor_value)
    maximum = jnp.max(scores, axis=2)
    weights = jnp.where(visible, jnp.exp(scores - maximum[:, :, None]), 0.0)
    weight_sum = jnp.sum(weights, axis=2)
    blended = jnp.einsum(
        "rqk,rkv->rqv",
        weights.astype(jnp.bfloat16),
        suffix[:, :, :KVR],
        preferred_element_type=jnp.float32,
    )
    flat_rows = queries_own.shape[0] * queries_own.shape[1]
    return (
        maximum.reshape(flat_rows),
        weight_sum.reshape(flat_rows),
        blended.reshape(flat_rows, KVR),
    )


def combine(first, second):
    maximum = jnp.maximum(first[0], second[0])
    scale_first = jnp.exp(first[0] - maximum)
    scale_second = jnp.exp(second[0] - maximum)
    weight_sum = first[1] * scale_first + second[1] * scale_second
    blended = first[2] * scale_first[:, None] + second[2] * scale_second[:, None]
    return (maximum, weight_sum, blended)


def per_device(queries, prefix_kv, suffix_kv, lengths):
    request_count, query_rows, latent_width = queries.shape
    first_key = lax.axis_index("row") * suffix_kv.shape[1]
    softmax_state = suffix_state(queries, suffix_kv, lengths, first_key)
    query_flat = queries.reshape(request_count * query_rows, latent_width)
    softmax_state = sweeper(
        query_flat, softmax_state, lax.all_gather(prefix_kv, "col", axis=0, tiled=True)
    )
    maximum, weight_sum, blended = merged(softmax_state, "row", combine)
    return (
        (blended / weight_sum[:, None]).astype(jnp.bfloat16).reshape(request_count, query_rows, KVR)
    )


END_FIRST = [("near", (0, 0, 0)), ("x", (0, 0, 1)), ("near", (0, 0, 1)), ("x", (0, 0, 0))]
END_EVENTS = [
    ((0, 1, 0), ["x"]),
    ((1, 0, 1), ["near"]),
    ((0, 1, 1), ["x"]),
    ((1, 0, 0), []),
    ((0, 2, 0), ["x"]),
    ((1, 1, 0), []),
    ((0, 2, 1), ["x"]),
    ((1, 1, 1), []),
    ((0, 3, 0), ["x"]),
    ((1, 2, 0), []),
    ((0, 3, 1), []),
    ((1, 2, 1), []),
    ((1, 3, 1), []),
    ((1, 3, 0), []),
]
MID_FIRST = [
    ("near", (0, 1, 0)), ("up", (0, 1, 0)), ("x", (0, 1, 1)),
    ("near", (0, 1, 1)), ("up", (0, 1, 1)), ("x", (0, 1, 0)),
]
MID_EVENTS = [
    ((0, 2, 0), ["near", "x"]),
    ((0, 0, 0), ["up", "x"]),
    ((1, 1, 1), []),
    ((0, 2, 1), ["near"]),
    ((0, 0, 1), ["up"]),
    ((1, 1, 0), []),
    ((0, 3, 0), ["near", "x"]),
    ((1, 0, 1), ["up", ("up", (1, 1, 1))]),
    ((1, 0, 0), []),
    ((0, 3, 1), ["near"]),
    ((1, 2, 0), []),
    ((1, 3, 1), ["near"]),
    ((1, 3, 0), []),
    ((1, 2, 1), []),
]
CHUNK = 256
LOG2E = 1.4426950408889634


def dot_t(a, b):
    return lax.dot_general(a, b, (((1,), (1,)), ((), ())), preferred_element_type=jnp.float32)


def gather_attend(
    q_hbm, prefix_hbm, suffix_hbm, lengths, out_hbm,
    q_flipped, q, keys, suffix, result, top, total, acc,
    local_sem, x_send, near_send, up_send, sib_send, recv, sib_recv, suf_send, suf_recv, out_send, out_recv,
):
    group, row, col = lax.axis_index("group"), lax.axis_index("row"), lax.axis_index("col")
    z, x = col // 2, col % 2
    flip = z // 2
    place = z + flip * (3 - 2 * z)
    at_end = place == 0
    unit = prefix_hbm.shape[1] // 2
    half_suffix = suffix_hbm.shape[2]
    other = 1 - row

    def line(p):
        return p + flip * (3 - 2 * p)

    def index(name):
        other_x, p, h = name
        return ((x + other_x - 2 * x * other_x) * 4 + line(p)) * 2 + h

    def slot(u, r):
        return keys.at[u, r]

    devices = {
        "x": (group, row, z * 2 + 1 - x),
        "end_near": (group, row, line(1) * 2 + x),
        "mid_near": (group, row, line(0) * 2 + x),
        "up": (group, row, line(2) * 2 + x),
    }
    sibling = (group, other, col)

    def remote(src, dst, send_sem, recv_sem, device):
        return pltpu.make_async_remote_copy(
            src_ref=src, dst_ref=dst, send_sem=send_sem, recv_sem=recv_sem,
            device_id=device, device_id_type=pl.DeviceIdType.MESH,
        )

    barrier = pltpu.get_barrier_semaphore()

    def greet(device):
        pl.semaphore_signal(barrier, inc=1, device_id=device, device_id_type=pl.DeviceIdType.MESH)

    greet(sibling)
    greet(devices["x"])

    q_in = pltpu.make_async_copy(q_hbm.at[row], q_flipped, local_sem.at[0])
    q_in.start()
    own_in = []
    for h in range(2):
        own_in.append(
            pltpu.make_async_copy(
                prefix_hbm.at[:, pl.ds(h * unit, unit)], slot(index_own(col, h, z, x), row), local_sem.at[1 + h]
            )
        )
        own_in[-1].start()
    suffix_in = pltpu.make_async_copy(suffix_hbm.at[row], suffix.at[row], local_sem.at[3])
    suffix_in.start()

    @pl.when(at_end)
    def _():
        greet(devices["end_near"])
        pl.semaphore_wait(barrier, 3)

    @pl.when(jnp.logical_not(at_end))
    def _():
        greet(devices["mid_near"])
        greet(devices["up"])
        pl.semaphore_wait(barrier, 4)

    sems = {"x": x_send, "near": near_send, "up": up_send}

    def make_send(kind, counts, link, name, from_hbm):
        at = counts[link]
        counts[link] += 1
        where = (kind + "_near") if link == "near" else link

        def build():
            u = index(name)
            src = prefix_hbm.at[:, pl.ds(name[2] * unit, unit)] if from_hbm else slot(u, row)
            return remote(src, slot(u, row), sems[link].at[at], recv.at[u], devices[where])

        return build

    def plan(kind, first, events):
        counts = {"x": 0, "near": 0, "up": 0}
        opening = [make_send(kind, counts, link, name, True) for link, name in first]
        after = []
        for name, links in events:
            sends = []
            for link in links:
                if isinstance(link, tuple):
                    sends.append(make_send(kind, counts, link[0], link[1], False))
                else:
                    sends.append(make_send(kind, counts, link, name, False))
            after.append(sends)
        return opening, after

    end_opening, end_after = plan("end", END_FIRST, END_EVENTS)
    mid_opening, mid_after = plan("mid", MID_FIRST, MID_EVENTS)

    def both(end_list, mid_list, act):
        if end_list:
            @pl.when(at_end)
            def _():
                for build in end_list:
                    act(build())
        if mid_list:
            @pl.when(jnp.logical_not(at_end))
            def _():
                for build in mid_list:
                    act(build())

    both(end_opening, mid_opening, lambda copy: copy.start())

    sib_sends = []
    own_units = [index_own(col, h, z, x) for h in range(2)]
    for h in range(2):
        copy = remote(
            prefix_hbm.at[:, pl.ds(h * unit, unit)], slot(own_units[h], row),
            sib_send.at[h], sib_recv.at[own_units[h]], sibling,
        )
        copy.start()
        sib_sends.append(copy)
    suffix_out = remote(suffix_hbm.at[other], suffix.at[row], suf_send, suf_recv, sibling)
    suffix_out.start()

    scale = softmax_scale * LOG2E
    top[...] = jnp.full(top.shape, floor_value, jnp.float32)
    total[...] = jnp.zeros(total.shape, jnp.float32)
    acc[...] = jnp.zeros(acc.shape, jnp.float32)
    length = lengths[row]

    def attend(block, first_key=None):
        scores = jnp.dot(q[...], block, preferred_element_type=jnp.float32) * scale
        if first_key is not None:
            shape = scores.shape
            key = first_key + lax.broadcasted_iota(jnp.int32, shape, 1)
            position = lax.broadcasted_iota(jnp.int32, shape, 0) // H
            scores = jnp.where(key < length - POS + 1 + position, scores, floor_value)
        before = top[...]
        now = jnp.maximum(before, jnp.max(scores, axis=1, keepdims=True))
        weights = jnp.exp2(scores - now)
        rescale = jnp.exp2(before - now)
        top[...] = now
        total[...] = total[...] * rescale + jnp.sum(weights, axis=1, keepdims=True)
        acc[...] = acc[...] * rescale + dot_t(weights.astype(jnp.bfloat16), block[:KVR, :])

    def attend_unit(u):
        attend(jnp.concatenate([keys[u, 0], keys[u, 1]], axis=1))

    def await_sibling(u):
        remote(slot(u, row), slot(u, other), sib_send.at[0], sib_recv.at[u], sibling).wait_recv()

    pieces = half_suffix // CHUNK

    def attend_suffix(i):
        if i == 0:
            suffix_in.wait()
        if i == pieces:
            remote(suffix.at[row], suffix.at[other], suf_send, suf_recv, sibling).wait_recv()
        part = row if i < pieces else other
        start = (i % pieces) * CHUNK
        attend(suffix[part, :, start : start + CHUNK], part * half_suffix + start)

    q_in.wait()
    q[...] = q_flipped[...].T
    for h in range(2):
        own_in[h].wait()
    for u in own_units:
        await_sibling(u)
        attend_unit(u)

    for i in range(4):
        attend_suffix(i)
    steps = len(END_EVENTS)
    names = []
    for k in range(steps):
        u = jnp.where(at_end, index(END_EVENTS[k][0]), index(MID_EVENTS[k][0]))
        remote(slot(u, row), slot(u, row), sib_send.at[0], recv.at[u], sibling).wait_recv()
        both(end_after[k], mid_after[k], lambda copy: copy.start())
        copy = remote(slot(u, row), slot(u, row), sib_send.at[2 + k], sib_recv.at[u], sibling)
        copy.start()
        sib_sends.append(copy)
        names.append(u)
        if k >= 4 and k < 12 - 4:
            attend_suffix(k - 4 + 4)
        if k >= 1:
            await_sibling(names[k - 1])
            attend_unit(names[k - 1])
    for i in range(steps, 2 * pieces):
        attend_suffix(i)
    await_sibling(names[-1])
    attend_unit(names[-1])

    result[...] = (acc[...] / total[...]).astype(jnp.bfloat16)
    final = remote(result, out_hbm.at[row], out_send, out_recv, sibling)
    final.start()
    keep = pltpu.make_async_copy(result, out_hbm.at[row], local_sem.at[4])
    keep.start()
    both(
        end_opening + [b for sends in end_after for b in sends],
        mid_opening + [b for sends in mid_after for b in sends],
        lambda copy: copy.wait_send(),
    )
    for copy in sib_sends:
        copy.wait_send()
    suffix_out.wait_send()
    keep.wait()
    final.wait_send()
    remote(result, out_hbm.at[other], out_send, out_recv, sibling).wait_recv()


def index_own(col, h, z, x):
    return (x * 4 + z) * 2 + h


def ring_device(queries, prefix_kv, suffix_kv, lengths):
    requests, query_rows, width = queries.shape
    unit = prefix_kv.shape[0] // 2
    half_suffix = suffix_kv.shape[1]
    dma = pltpu.SemaphoreType.DMA
    anywhere = pl.BlockSpec(memory_space=pl.ANY)
    return pl.pallas_call(
        gather_attend,
        out_shape=jax.ShapeDtypeStruct((requests, query_rows, KVR), jnp.bfloat16),
        in_specs=[anywhere, anywhere, anywhere, pl.BlockSpec(memory_space=pltpu.SMEM)],
        out_specs=anywhere,
        scratch_shapes=[
            pltpu.VMEM((width, query_rows), jnp.bfloat16),
            pltpu.VMEM((query_rows, width), jnp.bfloat16),
            pltpu.VMEM((16, 2, width, unit), jnp.bfloat16),
            pltpu.VMEM((2, width, half_suffix), jnp.bfloat16),
            pltpu.VMEM((query_rows, KVR), jnp.bfloat16),
            pltpu.VMEM((query_rows, 1), jnp.float32),
            pltpu.VMEM((query_rows, 1), jnp.float32),
            pltpu.VMEM((query_rows, KVR), jnp.float32),
            dma((5,)), dma((7,)), dma((7,)), dma((6,)), dma((16,)), dma((16,)), dma((16,)),
            dma, dma, dma, dma,
        ],
        compiler_params=pltpu.CompilerParams(
            collective_id=0, has_side_effects=True, vmem_limit_bytes=56 * 1024 * 1024
        ),
    )(jnp.swapaxes(queries, 1, 2), prefix_kv.T, jnp.swapaxes(suffix_kv, 1, 2), lengths)


def solution(mesh):
    small = dict(mesh.shape) == {"group": 2, "row": 2, "col": 8}
    return jax.shard_map(
        ring_device if small else per_device,
        mesh=mesh,
        in_specs=(
            P(("group", "col"), None, None),
            P(("group", "row", "col"), None),
            P(("group", "col"), "row", None),
            P(("group", "col")),
        ),
        out_specs=P(("group", "col"), None, None),
        check_vma=False,
    )
```

```python
import math

import jax
import jax.numpy as jnp
from jax import lax
from jax.experimental import pallas as pl
from jax.experimental.pallas import tpu as pltpu
from jax.sharding import PartitionSpec as P

H = 128
KVR = 512
POS = 2


softmax_scale = 192.0 ** (-0.5)
floor_value = -1e30


def merged(value, axis, join):
    pieces = jax.tree.map(lambda part: lax.all_gather(part, axis), value)
    head = jax.tree.map(lambda part: part[0], pieces)
    tail = jax.tree.map(lambda part: part[1:], pieces)
    subtotal, _ = lax.scan(lambda subtotal, share: (join(subtotal, share), None), head, tail)
    return subtotal


def absorb(running, query_flat, key_block):
    maximum, weight_sum, blended = running
    scores = (
        jnp.einsum("ml,kl->mk", query_flat, key_block, preferred_element_type=jnp.float32)
        * softmax_scale
    )
    new_max = jnp.maximum(maximum, jnp.max(scores, axis=1))
    weights = jnp.exp(scores - new_max[:, None])
    rescale = jnp.exp(maximum - new_max)
    weight_sum = weight_sum * rescale + jnp.sum(weights, axis=1)
    blended = blended * rescale[:, None] + jnp.dot(
        weights.astype(jnp.bfloat16), key_block[:, :KVR], preferred_element_type=jnp.float32
    )
    return (new_max, weight_sum, blended)


def sweeper(query_flat, running, key_piece):
    key_count = key_piece.shape[0]
    block_size = math.gcd(key_count, 512)
    pieces = key_piece.reshape(key_count // block_size, block_size, key_piece.shape[1])

    def scan_step(carried, key_block):
        return (absorb(carried, query_flat, key_block), None)

    return lax.scan(scan_step, running, pieces)[0]


def suffix_state(queries_own, suffix, lengths, first_key):
    scores = (
        jnp.einsum("rql,rkl->rqk", queries_own, suffix, preferred_element_type=jnp.float32)
        * softmax_scale
    )
    key_index = first_key + jnp.arange(suffix.shape[1], dtype=jnp.int32)
    position = jnp.arange(queries_own.shape[1], dtype=jnp.int32) // H
    key_limit = lengths[:, None] - POS + 1 + position[None, :]
    visible = key_index[None, None, :] < key_limit[:, :, None]
    scores = jnp.where(visible, scores, floor_value)
    maximum = jnp.max(scores, axis=2)
    weights = jnp.where(visible, jnp.exp(scores - maximum[:, :, None]), 0.0)
    weight_sum = jnp.sum(weights, axis=2)
    blended = jnp.einsum(
        "rqk,rkv->rqv",
        weights.astype(jnp.bfloat16),
        suffix[:, :, :KVR],
        preferred_element_type=jnp.float32,
    )
    flat_rows = queries_own.shape[0] * queries_own.shape[1]
    return (
        maximum.reshape(flat_rows),
        weight_sum.reshape(flat_rows),
        blended.reshape(flat_rows, KVR),
    )


def combine(first, second):
    maximum = jnp.maximum(first[0], second[0])
    scale_first = jnp.exp(first[0] - maximum)
    scale_second = jnp.exp(second[0] - maximum)
    weight_sum = first[1] * scale_first + second[1] * scale_second
    blended = first[2] * scale_first[:, None] + second[2] * scale_second[:, None]
    return (maximum, weight_sum, blended)


def per_device(queries, prefix_kv, suffix_kv, lengths):
    request_count, query_rows, latent_width = queries.shape
    first_key = lax.axis_index("row") * suffix_kv.shape[1]
    softmax_state = suffix_state(queries, suffix_kv, lengths, first_key)
    query_flat = queries.reshape(request_count * query_rows, latent_width)
    softmax_state = sweeper(
        query_flat, softmax_state, lax.all_gather(prefix_kv, "col", axis=0, tiled=True)
    )
    maximum, weight_sum, blended = merged(softmax_state, "row", combine)
    return (
        (blended / weight_sum[:, None]).astype(jnp.bfloat16).reshape(request_count, query_rows, KVR)
    )


END_FIRST = [("near", (0, 0, 0)), ("x", (0, 0, 1)), ("near", (0, 0, 1)), ("x", (0, 0, 0))]
END_EVENTS = [
    ((0, 1, 0), ["x"]),
    ((1, 0, 1), ["near"]),
    ((0, 1, 1), ["x"]),
    ((1, 0, 0), []),
    ((0, 2, 0), ["x"]),
    ((1, 1, 0), []),
    ((0, 2, 1), ["x"]),
    ((1, 1, 1), []),
    ((0, 3, 0), ["x"]),
    ((1, 2, 0), []),
    ((0, 3, 1), []),
    ((1, 2, 1), []),
    ((1, 3, 1), []),
    ((1, 3, 0), []),
]
MID_FIRST = [
    ("near", (0, 1, 0)), ("up", (0, 1, 0)), ("x", (0, 1, 1)),
    ("near", (0, 1, 1)), ("up", (0, 1, 1)), ("x", (0, 1, 0)),
]
MID_EVENTS = [
    ((0, 2, 0), ["near", "x"]),
    ((0, 0, 0), ["up", "x"]),
    ((1, 1, 1), []),
    ((0, 2, 1), ["near"]),
    ((0, 0, 1), ["up"]),
    ((1, 1, 0), []),
    ((0, 3, 0), ["near", "x"]),
    ((1, 0, 1), ["up", ("up", (1, 1, 1))]),
    ((1, 0, 0), []),
    ((0, 3, 1), ["near"]),
    ((1, 2, 0), []),
    ((1, 3, 1), ["near"]),
    ((1, 3, 0), []),
    ((1, 2, 1), []),
]
CHUNK = 256
LOG2E = 1.4426950408889634


def dot_t(a, b):
    return lax.dot_general(a, b, (((1,), (1,)), ((), ())), preferred_element_type=jnp.float32)


def gather_attend(
    q_hbm, prefix_hbm, suffix_hbm, lengths, out_hbm,
    q_flipped, q, keys, suffix, result, top, total, acc,
    local_sem, x_send, near_send, up_send, sib_send, recv, sib_recv, suf_send, suf_recv, out_send, out_recv,
):
    group, row, col = lax.axis_index("group"), lax.axis_index("row"), lax.axis_index("col")
    z, x = col // 2, col % 2
    flip = z // 2
    place = z + flip * (3 - 2 * z)
    at_end = place == 0
    unit = prefix_hbm.shape[1] // 2
    half_suffix = suffix_hbm.shape[2]
    other = 1 - row

    def line(p):
        return p + flip * (3 - 2 * p)

    def index(name):
        other_x, p, h = name
        return ((x + other_x - 2 * x * other_x) * 4 + line(p)) * 2 + h

    def slot(u, r):
        return keys.at[u, r]

    devices = {
        "x": (group, row, z * 2 + 1 - x),
        "end_near": (group, row, line(1) * 2 + x),
        "mid_near": (group, row, line(0) * 2 + x),
        "up": (group, row, line(2) * 2 + x),
    }
    sibling = (group, other, col)

    def remote(src, dst, send_sem, recv_sem, device):
        return pltpu.make_async_remote_copy(
            src_ref=src, dst_ref=dst, send_sem=send_sem, recv_sem=recv_sem,
            device_id=device, device_id_type=pl.DeviceIdType.MESH,
        )

    barrier = pltpu.get_barrier_semaphore()

    def greet(device):
        pl.semaphore_signal(barrier, inc=1, device_id=device, device_id_type=pl.DeviceIdType.MESH)

    greet(sibling)
    greet(devices["x"])

    q_in = pltpu.make_async_copy(q_hbm.at[row], q_flipped, local_sem.at[0])
    q_in.start()
    own_in = []
    for h in range(2):
        own_in.append(
            pltpu.make_async_copy(
                prefix_hbm.at[:, pl.ds(h * unit, unit)], slot(index_own(col, h, z, x), row), local_sem.at[1 + h]
            )
        )
        own_in[-1].start()
    suffix_in = pltpu.make_async_copy(suffix_hbm.at[row], suffix.at[row], local_sem.at[3])
    suffix_in.start()

    @pl.when(at_end)
    def _():
        greet(devices["end_near"])
        pl.semaphore_wait(barrier, 3)

    @pl.when(jnp.logical_not(at_end))
    def _():
        greet(devices["mid_near"])
        greet(devices["up"])
        pl.semaphore_wait(barrier, 4)

    sems = {"x": x_send, "near": near_send, "up": up_send}

    def make_send(kind, counts, link, name, from_hbm):
        at = counts[link]
        counts[link] += 1
        where = (kind + "_near") if link == "near" else link

        def build():
            u = index(name)
            src = prefix_hbm.at[:, pl.ds(name[2] * unit, unit)] if from_hbm else slot(u, row)
            return remote(src, slot(u, row), sems[link].at[at], recv.at[u], devices[where])

        return build

    def plan(kind, first, events):
        counts = {"x": 0, "near": 0, "up": 0}
        opening = [make_send(kind, counts, link, name, True) for link, name in first]
        after = []
        for name, links in events:
            sends = []
            for link in links:
                if isinstance(link, tuple):
                    sends.append(make_send(kind, counts, link[0], link[1], False))
                else:
                    sends.append(make_send(kind, counts, link, name, False))
            after.append(sends)
        return opening, after

    end_opening, end_after = plan("end", END_FIRST, END_EVENTS)
    mid_opening, mid_after = plan("mid", MID_FIRST, MID_EVENTS)

    def both(end_list, mid_list, act):
        if end_list:
            @pl.when(at_end)
            def _():
                for build in end_list:
                    act(build())
        if mid_list:
            @pl.when(jnp.logical_not(at_end))
            def _():
                for build in mid_list:
                    act(build())

    both(end_opening, mid_opening, lambda copy: copy.start())

    sib_sends = []
    own_units = [index_own(col, h, z, x) for h in range(2)]
    for h in range(2):
        copy = remote(
            prefix_hbm.at[:, pl.ds(h * unit, unit)], slot(own_units[h], row),
            sib_send.at[h], sib_recv.at[own_units[h]], sibling,
        )
        copy.start()
        sib_sends.append(copy)
    suffix_out = remote(suffix_hbm.at[other], suffix.at[row], suf_send, suf_recv, sibling)
    suffix_out.start()

    scale = softmax_scale * LOG2E
    top[...] = jnp.full(top.shape, floor_value, jnp.float32)
    total[...] = jnp.zeros(total.shape, jnp.float32)
    acc[...] = jnp.zeros(acc.shape, jnp.float32)
    length = lengths[row]

    def attend(block, first_key=None):
        scores = jnp.dot(q[...], block, preferred_element_type=jnp.float32) * scale
        if first_key is not None:
            shape = scores.shape
            key = first_key + lax.broadcasted_iota(jnp.int32, shape, 1)
            position = lax.broadcasted_iota(jnp.int32, shape, 0) // H
            scores = jnp.where(key < length - POS + 1 + position, scores, floor_value)
        before = top[...]
        now = jnp.maximum(before, jnp.max(scores, axis=1, keepdims=True))
        weights = jnp.exp2(scores - now)
        rescale = jnp.exp2(before - now)
        top[...] = now
        total[...] = total[...] * rescale + jnp.sum(weights, axis=1, keepdims=True)
        acc[...] = acc[...] * rescale + dot_t(weights.astype(jnp.bfloat16), block[:KVR, :])

    def attend_unit(u):
        attend(jnp.concatenate([keys[u, 0], keys[u, 1]], axis=1))

    def await_sibling(u):
        remote(slot(u, row), slot(u, other), sib_send.at[0], sib_recv.at[u], sibling).wait_recv()

    pieces = half_suffix // CHUNK

    def attend_suffix(i):
        if i == 0:
            suffix_in.wait()
        if i == pieces:
            remote(suffix.at[row], suffix.at[other], suf_send, suf_recv, sibling).wait_recv()
        part = row if i < pieces else other
        start = (i % pieces) * CHUNK
        attend(suffix[part, :, start : start + CHUNK], part * half_suffix + start)

    q_in.wait()
    q[...] = q_flipped[...].T
    for h in range(2):
        own_in[h].wait()
    for u in own_units:
        await_sibling(u)
        attend_unit(u)

    for i in range(4):
        attend_suffix(i)
    steps = len(END_EVENTS)
    names = []
    for k in range(steps):
        u = jnp.where(at_end, index(END_EVENTS[k][0]), index(MID_EVENTS[k][0]))
        remote(slot(u, row), slot(u, row), sib_send.at[0], recv.at[u], sibling).wait_recv()
        both(end_after[k], mid_after[k], lambda copy: copy.start())
        copy = remote(slot(u, row), slot(u, row), sib_send.at[2 + k], sib_recv.at[u], sibling)
        copy.start()
        sib_sends.append(copy)
        names.append(u)
        if k >= 8 and k < 12:
            attend_suffix(k - 4)
        if k >= 1:
            await_sibling(names[k - 1])
            attend_unit(names[k - 1])
    for i in range(steps, 2 * pieces):
        attend_suffix(i)
    await_sibling(names[-1])
    attend_unit(names[-1])

    result[...] = (acc[...] / total[...]).astype(jnp.bfloat16)
    final = remote(result, out_hbm.at[row], out_send, out_recv, sibling)
    final.start()
    keep = pltpu.make_async_copy(result, out_hbm.at[row], local_sem.at[4])
    keep.start()
    both(
        end_opening + [b for sends in end_after for b in sends],
        mid_opening + [b for sends in mid_after for b in sends],
        lambda copy: copy.wait_send(),
    )
    for copy in sib_sends:
        copy.wait_send()
    suffix_out.wait_send()
    keep.wait()
    final.wait_send()
    remote(result, out_hbm.at[other], out_send, out_recv, sibling).wait_recv()


def index_own(col, h, z, x):
    return (x * 4 + z) * 2 + h


def ring_device(queries, prefix_kv, suffix_kv, lengths):
    requests, query_rows, width = queries.shape
    unit = prefix_kv.shape[0] // 2
    half_suffix = suffix_kv.shape[1]
    dma = pltpu.SemaphoreType.DMA
    anywhere = pl.BlockSpec(memory_space=pl.ANY)
    return pl.pallas_call(
        gather_attend,
        out_shape=jax.ShapeDtypeStruct((requests, query_rows, KVR), jnp.bfloat16),
        in_specs=[anywhere, anywhere, anywhere, pl.BlockSpec(memory_space=pltpu.SMEM)],
        out_specs=anywhere,
        scratch_shapes=[
            pltpu.VMEM((width, query_rows), jnp.bfloat16),
            pltpu.VMEM((query_rows, width), jnp.bfloat16),
            pltpu.VMEM((16, 2, width, unit), jnp.bfloat16),
            pltpu.VMEM((2, width, half_suffix), jnp.bfloat16),
            pltpu.VMEM((query_rows, KVR), jnp.bfloat16),
            pltpu.VMEM((query_rows, 1), jnp.float32),
            pltpu.VMEM((query_rows, 1), jnp.float32),
            pltpu.VMEM((query_rows, KVR), jnp.float32),
            dma((5,)), dma((7,)), dma((7,)), dma((6,)), dma((16,)), dma((16,)), dma((16,)),
            dma, dma, dma, dma,
        ],
        compiler_params=pltpu.CompilerParams(
            collective_id=0, has_side_effects=True, vmem_limit_bytes=56 * 1024 * 1024
        ),
    )(jnp.swapaxes(queries, 1, 2), prefix_kv.T, jnp.swapaxes(suffix_kv, 1, 2), lengths)


def solution(mesh):
    small = dict(mesh.shape) == {"group": 2, "row": 2, "col": 8}
    return jax.shard_map(
        ring_device if small else per_device,
        mesh=mesh,
        in_specs=(
            P(("group", "col"), None, None),
            P(("group", "row", "col"), None),
            P(("group", "col"), "row", None),
            P(("group", "col")),
        ),
        out_specs=P(("group", "col"), None, None),
        check_vma=False,
    )
```
